256 devices in a mesh: cuts: 4 (over y_hi, core), fsdp: 64 (over y_lo, z, x).
Axes of the slice: x: 4, y: 4 (y_hi: 2, y_lo: 2; y = y_hi * 2 + y_lo), z: 8, core: 2. Of those that a mesh axis runs over, the one named last changes fastest.
Arguments:
- hidden_in: bfloat16 [65536, 8192], P(('cuts', 'fsdp')), may hold values from -24 to 24
- value_weight: bfloat16 [8192, 512], P('fsdp'), may hold values from -0.0625 to 0.0625
- queries: bfloat16 [65536, 4096], P(('cuts', 'fsdp')), may hold values from -100 to 100
- keys: bfloat16 [65536, 512], P(('cuts', 'fsdp')), may hold values from -5 to 5
- out_grad: bfloat16 [65536, 4096], P(('cuts', 'fsdp')), may hold values from -6 to 6
- new_logp: float32 [65536], P(('cuts', 'fsdp')), may hold values from -1.5 to -1
- old_logp: float32 [65536], P(('cuts', 'fsdp')), may hold values from -1.5 to -1
- rewards: float32 [256], P(('cuts', 'fsdp')), may hold values from -4 to 4
- resp_len: int32 [4, 64], P('cuts', 'fsdp'), may hold values from 1 to 256, 10240 in all within a row
- group_id: int32 [4, 64], P('cuts', 'fsdp'), may hold values from 0 to 7, never falling along the last dimension, each value on 1 to 16 neighbouring positions
Outputs:
- input_grad: bfloat16 [65536, 8192], P(('cuts', 'fsdp'))
- weight_grad: float32 [8192, 512], P('fsdp')
- clip_frac: float32 [], replicated
The draws below stay inside these ranges and needn't reach their ends.
Inputs may be any that keep to these rules, and one draw needn't show every extreme that they name: `group_id`: group ids never fall along a slice's responses.
All inputs are finite; a program needn't handle non-finite values. No bound on the sum of `resp_len` on one device may be relied on, other than what follows from the above.
Results may differ from the reference program's by a relative error of at most 0.014.
Values may be sent and summed in bfloat16 or wider, within the bound.
A program may use at most 128 MiB of HBM per device.

```python
import math
import jax
import jax.numpy as jnp
import numpy as np
from jax import lax

D = 8192
HEAD = 128
KV_HEADS = 4
GROUP = 8
LEN = 256
KW = 512
QW = 4096
SEQS = 256
TOKENS = 65536
GROUPS = 8
N_CUTS = 4
N_FSDP = 64


def keys_base(key):
    return jnp.clip(jax.random.normal(key, (TOKENS, KV_HEADS * HEAD), jnp.float32), -5.0, 5.0)


def draw_keys(key, part):
    base = keys_base(key)
    return base.astype(jnp.bfloat16)


def draw_queries(key, part):
    key = jax.random.fold_in(key, 11)
    values = jnp.clip(jax.random.normal(key, (TOKENS, KV_HEADS * GROUP * HEAD), jnp.float32), -5.0, 5.0)
    return values.astype(jnp.bfloat16)


def strengthened(result, rng, source, target, blocks, factor):
    def block_of(position):
        return (jnp.arange(result.shape[position]) // (result.shape[position] // blocks)).reshape((-1,) + (1,) * (result.ndim - 1 - position))

    first = jax.random.permutation(rng, blocks)[block_of(target)]
    far = (block_of(target) + blocks // 2) % blocks
    return jnp.where((block_of(source) == first) | (block_of(source) == far), factor * result, result)


def level_of(stream_key, shape, split, low, high):
    loudness = 1.0
    for dim, blocks in split:
        steps = jax.random.uniform(jax.random.fold_in(jax.random.fold_in(stream_key, 6), dim), (blocks,), jnp.float32, low / len(split), high / len(split))
        loudness = loudness * jnp.repeat(jnp.exp(steps), shape[dim] // blocks).reshape((-1,) + (1,) * (len(shape) - 1 - dim))
    return loudness


def profile(amount, total, bound, skew):
    weights = [(1 << 20) // math.isqrt(grade ** skew) + 1 for grade in range(2, amount + 1)]
    surplus, holding = total - bound - (amount - 1), [1] * (amount - 1)
    while surplus > 0:
        movable = [i for i in range(amount - 1) if holding[i] < bound]
        whole, budget = sum([weights[i] for i in movable]), surplus
        for i in movable:
            addition = min(bound - holding[i], max(1, budget * weights[i] // whole), surplus)
            holding[i] = holding[i] + addition
            surplus = surplus - addition
    return np.array([bound] + holding)


def ragged_sizes(key, number_of, total, limit, skew):
    if number_of == 2:
        one = jax.random.randint(key, (), max(1, total - limit), min(limit, total - 1) + 1)
        return jnp.stack([one, total - one])
    sizes = jnp.asarray(profile(number_of, total, limit, skew), jnp.int32)
    twos = (number_of - 1) // 2
    source_of, taker = sizes[1:1 + 2 * twos:2], sizes[2:2 + 2 * twos:2]
    slack = jnp.minimum(source_of - 1, limit - taker)
    moved = jax.random.randint(jax.random.fold_in(key, 1), (twos,), 0, 1 << 20) % (slack + 1)
    sizes = sizes.at[1:1 + 2 * twos:2].set(source_of - moved).at[2:2 + 2 * twos:2].set(taker + moved)
    return sizes[jax.random.permutation(jax.random.fold_in(key, 2), number_of)]


def gaussian(rng, shape, spread, limit, cuts=(), held_as=jnp.bfloat16):
    array = jax.random.normal(rng, shape, jnp.float32) * spread
    if len(cuts) > 0:
        array = level_of(rng, shape, cuts, -0.22, 0.18) * array
    return jnp.clip(array, min=-limit, max=limit).astype(held_as)


def noise_with(own_key, dims, scale, limit, cuts, heavy, kind=jnp.bfloat16):
    array = scale * jax.random.normal(own_key, dims, jnp.float32)
    if cuts:
        array = array * level_of(own_key, dims, cuts, -0.22, 0.18)
    return jnp.clip(strengthened(array, jax.random.fold_in(own_key, 3), *heavy), -limit, limit).astype(kind)


def setup_inputs(seed: int = 0) -> dict:
    seeds = jax.random.split(jax.random.key(seed), 11)
    return {
        "hidden_in": noise_with(seeds[0], (TOKENS, D), 1.0, 24.0, ((0, 256),), (0, 1, 256, 6.0)),
        "value_weight": gaussian(seeds[1], (D, KW), D ** -0.5, 0.0625, ((0, 64),)),
        "queries": draw_queries(jax.random.fold_in(seeds[10], 71), 0),
        "keys": draw_keys(jax.random.fold_in(seeds[10], 71), 0),
        "out_grad": gaussian(seeds[4], (TOKENS, QW), 1.0, 6.0, ((0, 256),)),
        "new_logp": jnp.clip(-1.5 + 0.5 * jax.random.uniform(seeds[5], (TOKENS,), jnp.float32) ** level_of(seeds[5], (TOKENS,), ((0, 256),), -0.2, 0.2), -1.5, -1.0),
        "old_logp": jnp.clip(-1.5 + 0.5 * jax.random.uniform(seeds[6], (TOKENS,), jnp.float32) ** level_of(seeds[6], (TOKENS,), ((0, 256),), -0.2, 0.2), -1.5, -1.0),
        "rewards": gaussian(seeds[7], (SEQS,), 1.0, 4.0, ((0, 256),), jnp.float32),
        "resp_len": jax.vmap(lambda own: ragged_sizes(own, N_FSDP, N_FSDP * LEN * 5 // 8, LEN, 1))(jax.random.split(seeds[8], N_CUTS)).reshape((N_CUTS, N_FSDP)).astype(jnp.int32),
        "group_id": jax.vmap(lambda own: jnp.searchsorted(jnp.cumsum(ragged_sizes(own, GROUPS, N_FSDP, 16, 0)), jnp.arange(N_FSDP), side="right"))(jax.random.split(seeds[9], N_CUTS)).reshape((N_CUTS, N_FSDP)).astype(jnp.int32),
    }


def value_grad(query_seq, key_seq, dout_seq):
    scale = 1.0 / HEAD ** 0.5
    rows = jnp.arange(LEN)
    allowed = rows[None, :] <= rows[:, None]
    query_heads = query_seq.reshape(LEN, KV_HEADS, GROUP, HEAD)
    key_heads = key_seq.reshape(LEN, KV_HEADS, HEAD)
    dout_heads = dout_seq.reshape(LEN, KV_HEADS, GROUP, HEAD)
    pieces = []
    for head in range(KV_HEADS):
        scores = jnp.einsum('igd,jd->gij', query_heads[:, head].astype(jnp.float32), key_heads[:, head].astype(jnp.float32)) * scale
        scores = jnp.where(allowed[None], scores, -1e+30)
        top = lax.optimization_barrier(jnp.max(scores, axis=2, keepdims=True))
        expo = jnp.exp(scores - top)
        probs = (expo / lax.optimization_barrier(jnp.sum(expo, axis=2, keepdims=True))).astype(jnp.bfloat16)
        pieces.append(jnp.einsum('gij,igd->jd', probs.astype(jnp.float32), dout_heads[:, head].astype(jnp.float32)))
    return jnp.concatenate(pieces, axis=1).astype(jnp.bfloat16)

def reference(hidden_in, value_weight, queries, keys, out_grad, new_logp, old_logp, rewards, resp_len, group_id):
    lengths = resp_len.reshape(-1)
    groups = group_id.reshape(-1)
    seq_index = jnp.arange(SEQS)
    slot_key = seq_index // N_FSDP * GROUPS + groups
    table = (slot_key[:, None] == jnp.arange(N_CUTS * GROUPS)[None, :]).astype(jnp.float32)
    cnt = lax.optimization_barrier(jnp.sum(table, axis=0))
    sum_one = lax.optimization_barrier(jnp.sum(table * rewards[:, None], axis=0))
    sum_two = lax.optimization_barrier(jnp.sum(table * (rewards * rewards)[:, None], axis=0))
    own_cnt = lax.optimization_barrier(jnp.sum(table * cnt[None, :], axis=1))
    own_one = lax.optimization_barrier(jnp.sum(table * sum_one[None, :], axis=1))
    own_two = lax.optimization_barrier(jnp.sum(table * sum_two[None, :], axis=1))
    mean = own_one / own_cnt
    var = own_two / own_cnt - mean * mean
    adv_seq = (rewards - mean) / jnp.sqrt(var + 0.25)
    positions = jnp.arange(TOKENS) % LEN
    live = (positions.reshape(SEQS, LEN) < lengths[:, None]).astype(jnp.float32).reshape(-1)
    adv = jnp.repeat(adv_seq, LEN)
    ratio = jnp.exp(new_logp - old_logp)
    outside = jnp.logical_or(ratio > 1.28, ratio < 0.8).astype(jnp.float32)
    total = jnp.sum(live)
    clip_frac = jnp.sum(live * outside) / total
    active = jnp.where(adv > 0, ratio < 1.28, ratio > 0.8).astype(jnp.float32)
    coef = -live * adv * ratio * active * (TOKENS / total)
    dout = (coef[:, None] * out_grad.astype(jnp.float32)).astype(jnp.bfloat16)
    dvalue = lax.map(lambda items: value_grad(items[0], items[1], items[2]), (queries.reshape(SEQS, LEN, QW), keys.reshape(SEQS, LEN, KW), dout.reshape(SEQS, LEN, QW)))
    dvalue = dvalue.reshape(TOKENS, KW)
    input_grad = lax.dot_general(dvalue, value_weight, (((1,), (1,)), ((), ())), preferred_element_type=jnp.float32).astype(jnp.bfloat16)
    weight_grad = lax.dot_general(hidden_in, dvalue, (((0,), (0,)), ((), ())), preferred_element_type=jnp.float32)
    return (input_grad, weight_grad, clip_frac)
```

```python
import functools

import jax
import jax.numpy as jnp
from jax import lax
from jax.experimental import pallas as pl
from jax.experimental.pallas import tpu as pltpu
from jax.sharding import PartitionSpec as P

HEAD = 128
KV_HEADS = 4
GROUP = 8
LEN = 256
D = 8192
F32 = jnp.float32
BF16 = jnp.bfloat16
MESH = pl.DeviceIdType.MESH
N_X, N_Y, N_Z = 4, 4, 8
RA, RB, RC = 48, 32, 48
SLOTS = 192


def _coords():
    cuts = lax.axis_index("cuts")
    fsdp = lax.axis_index("fsdp")
    core = cuts % 2
    y_hi = cuts // 2
    y_lo = fsdp // 32
    z = (fsdp // 4) % 8
    x = fsdp % 4
    return x, y_hi * 2 + y_lo, z, core


def _device(x, y, z, core):
    return ((y // 2) * 2 + core, (y % 2) * 32 + z * 4 + x)


def _nt(a, b):
    return lax.dot_general(a, b, (((1,), (1,)), ((), ())), preferred_element_type=F32)


def _nn(a, b):
    return lax.dot_general(a, b, (((1,), (0,)), ((), ())), preferred_element_type=F32)


def kernel(
    hid, w, q, k, og, nlp, olp, rew, rlen, gid,
    ig, wg, cf,
    hv, qv, ogv, pt, douts, dvs, dvr, dvt, W, out,
    PA, PB, PC, rax, ray, raz, rcy, rcx, rcz, rbz, rbx, rby,
    fin, st, rsz, rsx, rsy, rsc, coefv,
    ssem, rsem, lsem, osem,
):
    x, y, z, c = _coords()
    y_lo, y_hi = y % 2, y // 2

    def xs(d):
        return (x + d + N_X) % N_X

    def ys(d):
        return (y + d + N_Y) % N_Y

    def zs(d):
        return (z + d + N_Z) % N_Z

    def at_x(d):
        return _device(xs(d), y, z, c)

    def at_y(d):
        return _device(x, ys(d), z, c)

    def at_z(d):
        return _device(x, y, zs(d), c)

    partner = _device(x, y, z, 1 - c)
    sent = []

    def send(src, dst, device):
        i = len(sent)
        copy = pltpu.make_async_remote_copy(
            src_ref=src, dst_ref=dst, send_sem=ssem.at[i], recv_sem=rsem.at[i],
            device_id=device, device_id_type=MESH,
        )
        copy.start()
        sent.append(copy)
        return copy

    loads = [
        pltpu.make_async_copy(q, qv, lsem.at[0]),
        pltpu.make_async_copy(og, ogv, lsem.at[1]),
        pltpu.make_async_copy(hid, hv.at[0], lsem.at[2]),
    ]
    for load in loads:
        load.start()

    barrier = pltpu.get_barrier_semaphore()
    around = [at_x(1), at_x(-1), at_x(2), at_y(1), at_y(-1), at_y(2), partner]
    around += [at_z(d) for d in range(1, 8)]
    around += [_device(x, ys(2), z, 1 - c)]
    for device in around:
        pl.semaphore_signal(barrier, inc=1, device_id=device, device_id_type=MESH)

    W[c, y_lo, z, x] = w[pl.ds(pl.multiple_of(64 * c, 64), 64), :]
    lane = lax.broadcasted_iota(jnp.int32, (8, 128), 1)
    group = gid[...]
    reward = rew[...]
    length = rlen[...].astype(F32)
    position = lax.broadcasted_iota(jnp.int32, (1, LEN), 1)
    live = (position < rlen[...]).astype(F32)
    ratio = jnp.exp(nlp[...] - olp[...])
    outside = jnp.logical_or(ratio > 1.28, ratio < 0.8).astype(F32)
    clipped = jnp.sum(live * outside, axis=1, keepdims=True)
    member = (lane % 8 == group).astype(F32)
    stats = jnp.where(
        lane < 8, member,
        jnp.where(
            lane < 16, member * reward,
            jnp.where(
                lane < 24, member * (reward * reward),
                jnp.where(lane == 24, length, jnp.where(lane == 25, clipped, 0.0)),
            ),
        ),
    )
    st[0] = stats
    pl.semaphore_wait(barrier, len(around))

    def stats_steps():
        copies = [send(st.at[0], rsz.at[d - 1], at_z(d)) for d in range(1, 8)]
        yield
        for copy in copies:
            copy.wait_recv()
        total = st[0]
        for i in range(7):
            total = total + rsz[i]
        st[1] = total
        copies = [send(st.at[1], rsx.at[d - 1], at_x(d)) for d in range(1, 4)]
        yield
        for copy in copies:
            copy.wait_recv()
        st[2] = (st[1] + rsx[0]) + (rsx[1] + rsx[2])
        other = _device(x, y_hi * 2 + (1 - y_lo), z, c)
        copy = send(st.at[2], rsy, other)
        yield
        copy.wait_recv()
        st[3] = st[2] + rsy[...]
        copies = [
            send(st.at[3], rsc.at[0], at_y(2)),
            send(st.at[3], rsc.at[1], partner),
            send(st.at[3], rsc.at[2], _device(x, ys(2), z, 1 - c)),
        ]
        yield
        for copy in copies:
            copy.wait_recv()
        every = ((st[3] + rsc[0]) + (rsc[1] + rsc[2]))[0:1]
        top = lane[0:1]
        all_live = jnp.sum(jnp.where(top == 24, every, 0.0), axis=1, keepdims=True)
        all_out = jnp.sum(jnp.where(top == 25, every, 0.0), axis=1, keepdims=True)
        cf[...] = all_out / all_live

    def ring_z(view, half):
        up = send(view(z), view(z), at_z(1))
        down = send(view(z), view(z), at_z(-1))
        yield
        for d in (1, 2, 3):
            up.wait_recv()
            down.wait_recv()
            if d < 3:
                up = send(view(zs(-d)), view(zs(-d)), at_z(1))
                down = send(view(zs(d)), view(zs(d)), at_z(-1))
            else:
                up = send(half(zs(-3), 0), half(zs(-3), 0), at_z(1))
                down = send(half(zs(3), 1), half(zs(3), 1), at_z(-1))
            yield
        up.wait_recv()
        down.wait_recv()

    forwards = []

    def gather_a():
        own = W.at[c, y_lo, z, x, pl.ds(0, 16)]
        copy = send(own, own, at_y(1))
        yield
        copy.wait_recv()
        yield from ring_z(
            lambda i: W.at[c, :, i, x, pl.ds(0, 16)],
            lambda i, h: W.at[c, h, i, x, pl.ds(0, 16)],
        )

        def view(i):
            return W.at[c, :, :, i, pl.ds(0, 16)]

        def half(i, h):
            return W.at[c, h, :, i, pl.ds(0, 16)]

        up = send(view(x), view(x), at_x(1))
        down = send(view(x), view(x), at_x(-1))
        forwards.append(send(view(x), view(x), partner))
        yield
        up.wait_recv()
        down.wait_recv()
        up = send(half(xs(-1), 0), half(xs(-1), 0), at_x(1))
        down = send(half(xs(1), 1), half(xs(1), 1), at_x(-1))
        forwards.append(send(view(xs(-1)), view(xs(-1)), partner))
        forwards.append(send(view(xs(1)), view(xs(1)), partner))
        yield
        up.wait_recv()
        down.wait_recv()
        forwards.append(send(view(xs(2)), view(xs(2)), partner))

    def gather_b():
        own = W.at[c, y_lo, z, x, pl.ds(16, 16)]
        copies = [send(own, own, at_x(d)) for d in (1, 2, 3)]
        yield
        for copy in copies:
            copy.wait_recv()
        left = W.at[c, y_lo, z, pl.ds(0, 2), pl.ds(16, 16)]
        right = W.at[c, y_lo, z, pl.ds(2, 2), pl.ds(16, 16)]
        copies = [send(left, left, at_y(1)), send(right, right, at_y(-1))]
        yield
        for copy in copies:
            copy.wait_recv()
        def view(i):
            return W.at[c, :, i, :, pl.ds(16, 16)]

        yield from ring_z(view, lambda i, h: W.at[c, h, i, :, pl.ds(16, 16)])
        whole = W.at[c, :, :, :, pl.ds(16, 16)]
        forwards.append(send(whole, whole, partner))

    def gather_c():
        yield from ring_z(
            lambda i: W.at[c, y_lo, i, x, pl.ds(32, 32)],
            lambda i, h: W.at[c, y_lo, i, x, pl.ds(32 + 16 * h, 16)],
        )
        final = []

        def view(i):
            return W.at[c, y_lo, :, i, pl.ds(32, 32)]

        def half(i, h):
            return W.at[c, y_lo, pl.ds(4 * h, 4), i, pl.ds(32, 32)]

        def across(i):
            final.append(send(half(i, 0), half(i, 0), at_y(1)))
            final.append(send(half(i, 1), half(i, 1), at_y(-1)))

        up = send(view(x), view(x), at_x(1))
        down = send(view(x), view(x), at_x(-1))
        across(x)
        yield
        up.wait_recv()
        down.wait_recv()
        up = send(half(xs(-1), 0), half(xs(-1), 0), at_x(1))
        down = send(half(xs(1), 1), half(xs(1), 1), at_x(-1))
        across(xs(-1))
        across(xs(1))
        yield
        up.wait_recv()
        down.wait_recv()
        across(xs(2))
        mine = W.at[c, y_lo, :, :, pl.ds(32, 32)]
        forwards.append(send(mine, mine, partner))
        yield
        for copy in final:
            copy.wait_recv()
        theirs = W.at[c, 1 - y_lo, :, :, pl.ds(32, 32)]
        forwards.append(send(theirs, theirs, partner))

    def advance(steps):
        for step in list(steps):
            if next(step, "end") == "end":
                steps.remove(step)

    stat = [stats_steps()]
    gather = [gather_a(), gather_b(), gather_c()]
    advance(stat)
    advance(gather)
    hidden_copy = send(hid, hv.at[1], partner)

    loads[0].wait()
    factor = (1.0 / HEAD**0.5) * 1.4426950408889634
    row = lax.broadcasted_iota(jnp.int32, (HEAD, HEAD), 0)
    col = lax.broadcasted_iota(jnp.int32, (HEAD, HEAD), 1)
    causal = row <= col

    def soft(scores):
        top = jnp.max(scores, axis=0, keepdims=True)
        expo = jnp.exp2((scores - top) * factor)
        return (expo * (1.0 / jnp.sum(expo, axis=0, keepdims=True))).astype(BF16)

    def attend(head, first):
        keys = k[:, head * HEAD:(head + 1) * HEAD]

        def one(i, carry):
            g = first + i
            n = head * GROUP + g
            query = qv[:, pl.ds(pl.multiple_of(n * HEAD, HEAD), HEAD)]
            early = jnp.where(causal, _nt(keys[:128], query[:128]), -1e30)
            late = _nt(keys, query[128:])
            late = jnp.concatenate([late[:128], jnp.where(causal, late[128:], -1e30)], axis=0)
            at = pl.multiple_of(g * LEN, LEN)
            pt[head, pl.ds(0, 128), pl.ds(at, 128)] = soft(early)
            pt[head, pl.ds(128, 128), pl.ds(at, 128)] = jnp.zeros((128, 128), BF16)
            pt[head, :, pl.ds(at + 128, 128)] = soft(late)
            return carry

        lax.fori_loop(0, 4, one, 0)

    for part in range(8):
        attend(part // 2, 4 * (part % 2))
        advance(stat)
        advance(gather)

    slice_total = st[3][0:1]
    top = lane[0:1]

    def pick(at):
        return jnp.sum(jnp.where(top == at, slice_total, 0.0), axis=1, keepdims=True)

    own_cnt, own_one, own_two = pick(group), pick(8 + group), pick(16 + group)
    mean = own_one / own_cnt
    var = own_two / own_cnt - mean * mean
    adv = (reward - mean) / jnp.sqrt(var + 0.25)
    total = pick(24) * 4.0
    active = jnp.where(adv > 0, (ratio < 1.28).astype(F32), (ratio > 0.8).astype(F32))
    coef = -live * adv * ratio * active * (65536.0 / total)
    diagonal = lax.broadcasted_iota(jnp.int32, (LEN, LEN), 0) == lax.broadcasted_iota(jnp.int32, (LEN, LEN), 1)
    coefv[...] = jnp.broadcast_to(
        jnp.sum(jnp.where(diagonal, coef, 0.0), axis=1, keepdims=True), (LEN, HEAD)
    )
    loads[1].wait()
    for head in range(KV_HEADS):
        for g in range(GROUP):
            n = head * GROUP + g
            douts[g * LEN:(g + 1) * LEN, :] = (
                coefv[...] * ogv[:, n * HEAD:(n + 1) * HEAD].astype(F32)
            ).astype(BF16)
        dvs[head // 2, :, (head % 2) * HEAD:(head % 2 + 1) * HEAD] = _nn(pt[head], douts[...]).astype(BF16)
    dv_copy = send(dvs.at[1 - c], dvr, partner)
    advance(gather)
    loads[2].wait()
    hidden_copy.wait_recv()
    dvt[:, 0:LEN] = dvs[c].T
    dv_copy.wait_recv()
    dvt[:, LEN:2 * LEN] = dvr[...].T

    def partial(t, carry):
        yl, zz = t // 8, t % 8
        columns = pl.ds(pl.multiple_of(t * 512, 512), 512)
        block = _nn(dvt[:, 0:LEN], hv[0, :, columns]) + _nn(dvt[:, LEN:2 * LEN], hv[1, :, columns])
        block = block.astype(BF16)
        for i in range(N_X):
            b = block[:, i * 128:(i + 1) * 128]
            PA[yl, zz, i, 0] = b[0:48]
            PA[yl, zz, i, 1] = b[48:96]
            PB[yl, zz, i, 0] = b[96:128]
            PB[yl, zz, i, 1] = b[128:160]
            PC[yl, zz, i, 0] = b[160:208]
            PC[yl, zz, i, 1] = b[208:256]
        return carry

    lax.fori_loop(0, 16, partial, 0)

    def added(*terms):
        total = terms[0].astype(F32)
        for term in terms[1:]:
            total = total + term.astype(F32)
        return total

    def reduce_a():
        up = send(PA.at[:, :, xs(2), 0], rax.at[0], at_x(1))
        down = send(PA.at[:, :, xs(2), 1], rax.at[1], at_x(-1))
        up_b = send(PA.at[:, :, xs(1), 1], rax.at[2], at_x(1))
        down_b = send(PA.at[:, :, xs(-1), 0], rax.at[3], at_x(-1))
        yield
        up.wait_recv()
        PA[:, :, xs(1), 0] = added(PA[:, :, xs(1), 0], rax[0]).astype(BF16)
        up = send(PA.at[:, :, xs(1), 0], rax.at[4], at_x(1))
        down.wait_recv()
        PA[:, :, xs(-1), 1] = added(PA[:, :, xs(-1), 1], rax[1]).astype(BF16)
        down = send(PA.at[:, :, xs(-1), 1], rax.at[5], at_x(-1))
        yield
        up_b.wait_recv()
        down_b.wait_recv()
        up.wait_recv()
        down.wait_recv()
        PA[:, :, x, 0] = added(PA[:, :, x, 0], rax[3], rax[4]).astype(BF16)
        PA[:, :, x, 1] = added(PA[:, :, x, 1], rax[2], rax[5]).astype(BF16)
        copies = [send(PA.at[ys(d) % 2, :, x, ys(d) // 2], ray.at[d - 1], at_y(d)) for d in (2, 1, 3)]
        yield
        for copy in copies:
            copy.wait_recv()
        PA[y_lo, :, x, y_hi] = added(PA[y_lo, :, x, y_hi], ray[0], ray[1], ray[2]).astype(BF16)
        copies = [send(PA.at[y_lo, zs(d), x, y_hi], raz.at[d - 1], at_z(d)) for d in (4, 3, 5, 2, 6, 1, 7)]
        yield
        for copy in copies:
            copy.wait_recv()
        fin[y_hi, c, pl.ds(0, RA)] = added(PA[y_lo, z, x, y_hi], *[raz[i] for i in range(7)]).astype(BF16)

    def reduce_c():
        def view(d, h):
            return PC.at[ys(d) % 2, pl.ds(4 * h, 4), :, ys(d) // 2]

        def get(d, h):
            return PC[ys(d) % 2, pl.ds(4 * h, 4), :, ys(d) // 2]

        def put(d, h, value):
            PC[ys(d) % 2, pl.ds(4 * h, 4), :, ys(d) // 2] = value.astype(BF16)

        up = send(view(2, 0), rcy.at[0], at_y(1))
        down = send(view(2, 1), rcy.at[1], at_y(-1))
        up_b = send(view(1, 1), rcy.at[2], at_y(1))
        down_b = send(view(-1, 0), rcy.at[3], at_y(-1))
        yield
        up.wait_recv()
        put(1, 0, added(get(1, 0), rcy[0]))
        up = send(view(1, 0), rcy.at[4], at_y(1))
        down.wait_recv()
        put(-1, 1, added(get(-1, 1), rcy[1]))
        down = send(view(-1, 1), rcy.at[5], at_y(-1))
        yield
        up_b.wait_recv()
        down_b.wait_recv()
        up.wait_recv()
        down.wait_recv()
        put(0, 0, added(get(0, 0), rcy[3], rcy[4]))
        put(0, 1, added(get(0, 1), rcy[2], rcy[5]))
        copies = [send(PC.at[y_lo, :, xs(d), y_hi], rcx.at[d - 1], at_x(d)) for d in (2, 1, 3)]
        yield
        for copy in copies:
            copy.wait_recv()
        PC[y_lo, :, x, y_hi] = added(PC[y_lo, :, x, y_hi], rcx[0], rcx[1], rcx[2]).astype(BF16)
        copies = [send(PC.at[y_lo, zs(d), x, y_hi], rcz.at[d - 1], at_z(d)) for d in (4, 3, 5, 2, 6, 1, 7)]
        yield
        for copy in copies:
            copy.wait_recv()
        fin[y_hi, c, pl.ds(RA + RB, RC)] = added(
            PC[y_lo, z, x, y_hi], *[rcz[i] for i in range(7)]
        ).astype(BF16)

    def reduce_b():
        up = send(PB.at[:, zs(4), :, 0], rbz.at[0, :, :, 0], at_z(1))
        down = send(PB.at[:, zs(4), :, 1], rbz.at[0, :, :, 1], at_z(-1))
        yield
        up.wait_recv()
        PB[:, zs(3), :, 0] = added(PB[:, zs(3), :, 0], rbz[0, :, :, 0]).astype(BF16)
        up = send(PB.at[:, zs(3)], rbz.at[1], at_z(1))
        down.wait_recv()
        PB[:, zs(-3), :, 1] = added(PB[:, zs(-3), :, 1], rbz[0, :, :, 1]).astype(BF16)
        down = send(PB.at[:, zs(-3)], rbz.at[2], at_z(-1))
        yield
        for d in (2, 1):
            up.wait_recv()
            PB[:, zs(d)] = added(PB[:, zs(d)], rbz[5 - 2 * d]).astype(BF16)
            up = send(PB.at[:, zs(d)], rbz.at[7 - 2 * d], at_z(1))
            down.wait_recv()
            PB[:, zs(-d)] = added(PB[:, zs(-d)], rbz[6 - 2 * d]).astype(BF16)
            down = send(PB.at[:, zs(-d)], rbz.at[8 - 2 * d], at_z(-1))
            yield
        up.wait_recv()
        down.wait_recv()
        PB[:, z] = added(PB[:, z], rbz[5], rbz[6]).astype(BF16)
        copies = [send(PB.at[:, z, xs(d)], rbx.at[d - 1], at_x(d)) for d in (2, 1, 3)]
        yield
        for copy in copies:
            copy.wait_recv()
        PB[:, z, x] = added(PB[:, z, x], rbx[0], rbx[1], rbx[2]).astype(BF16)
        copies = [send(PB.at[ys(d) % 2, z, x, ys(d) // 2], rby.at[d - 1], at_y(d)) for d in (2, 1, 3)]
        yield
        for copy in copies:
            copy.wait_recv()
        fin[y_hi, c, pl.ds(RA, RB)] = added(PB[y_lo, z, x, y_hi], rby[0], rby[1], rby[2]).astype(BF16)

    scatter = [reduce_a(), reduce_c(), reduce_b()]
    advance(scatter)
    while gather:
        advance(gather)
        advance(scatter)
    for copy in forwards:
        copy.wait_recv()

    dv = jnp.concatenate([dvs[0], dvs[1]], axis=1)

    def stored(t):
        columns = pl.ds(pl.multiple_of(t * 512, 512), 512)
        return pltpu.make_async_copy(out.at[:, columns], ig.at[:, columns], osem.at[t])

    def product(t, carry):
        yl, zz = t // 8, t % 8
        rows = jnp.concatenate([W[h, yl, zz, i] for i in range(N_X) for h in range(2)], axis=0)
        out[:, pl.ds(pl.multiple_of(t * 512, 512), 512)] = _nt(dv, rows).astype(BF16)
        stored(t).start()
        return carry

    lax.fori_loop(0, 16, product, 0)

    while scatter:
        advance(scatter)
    mine = fin.at[y_hi, c]
    copies = [
        send(mine, mine, at_y(2)),
        send(mine, mine, partner),
        send(mine, mine, _device(x, ys(2), z, 1 - c)),
    ]
    for copy in copies:
        copy.wait_recv()
    pieces = []
    for core in range(2):
        for first, size in ((0, RA), (RA, RB), (RA + RB, RC)):
            for half in range(2):
                pieces.append(fin[half, core, pl.ds(first, size)])
    wg[...] = jnp.concatenate(pieces, axis=0).astype(F32).T

    while stat:
        advance(stat)

    def waited(t, carry):
        stored(t).wait()
        return carry

    lax.fori_loop(0, 16, waited, 0)
    for copy in sent:
        copy.wait_send()


def local(
    hidden_in, value_weight, queries, keys, out_grad, new_logp, old_logp, rewards, resp_len, group_id
):
    vmem = pl.BlockSpec(memory_space=pltpu.VMEM)
    hbm = pl.BlockSpec(memory_space=pl.ANY)
    bf = functools.partial(pltpu.VMEM, dtype=BF16)
    scratch = [
        bf((2, LEN, D)),
        bf((LEN, 4096)),
        bf((LEN, 4096)),
        bf((KV_HEADS, LEN, GROUP * LEN)),
        bf((GROUP * LEN, HEAD)),
        bf((2, LEN, 256)),
        bf((LEN, 256)),
        bf((256, 2 * LEN)),
        bf((2, 2, 8, 4, 64, 512)),
        bf((LEN, D)),
        bf((2, 8, 4, 2, RA, 128)),
        bf((2, 8, 4, 2, RB, 128)),
        bf((2, 8, 4, 2, RC, 128)),
        bf((6, 2, 8, RA, 128)),
        bf((3, 8, RA, 128)),
        bf((7, RA, 128)),
        bf((6, 4, 4, RC, 128)),
        bf((3, 8, RC, 128)),
        bf((7, RC, 128)),
        bf((7, 2, 4, 2, RB, 128)),
        bf((3, 2, 2, RB, 128)),
        bf((3, RB, 128)),
        bf((2, 2, 128, 128)),
        pltpu.VMEM((4, 8, 128), F32),
        pltpu.VMEM((7, 8, 128), F32),
        pltpu.VMEM((3, 8, 128), F32),
        pltpu.VMEM((8, 128), F32),
        pltpu.VMEM((3, 8, 128), F32),
        pltpu.VMEM((LEN, HEAD), F32),
        pltpu.SemaphoreType.DMA((SLOTS,)),
        pltpu.SemaphoreType.DMA((SLOTS,)),
        pltpu.SemaphoreType.DMA((3,)),
        pltpu.SemaphoreType.DMA((16,)),
    ]
    input_grad, weight_grad, clip_frac = pl.pallas_call(
        kernel,
        out_shape=(
            jax.ShapeDtypeStruct((LEN, D), BF16),
            jax.ShapeDtypeStruct((128, 512), F32),
            jax.ShapeDtypeStruct((1, 1), F32),
        ),
        in_specs=[hbm, vmem, hbm, vmem, hbm, vmem, vmem, vmem, vmem, vmem],
        out_specs=(hbm, vmem, vmem),
        scratch_shapes=scratch,
        compiler_params=pltpu.CompilerParams(
            collective_id=0, has_side_effects=True, vmem_limit_bytes=56 << 20
        ),
        name="value_backward",
    )(
        hidden_in, value_weight, queries, keys, out_grad,
        new_logp.reshape(1, LEN), old_logp.reshape(1, LEN), rewards.reshape(1, 1), resp_len, group_id,
    )
    return input_grad, weight_grad, clip_frac.reshape(())


def solution(mesh):
    rows = P(("cuts", "fsdp"), None)
    flat = P(("cuts", "fsdp"))
    return jax.shard_map(
        local,
        mesh=mesh,
        in_specs=(
            rows, P("fsdp", None), rows, rows, rows, flat, flat, flat, P("cuts", "fsdp"), P("cuts", "fsdp"),
        ),
        out_specs=(rows, P("fsdp", None), P()),
        check_vma=False,
    )
```

```python
import functools

import jax
import jax.numpy as jnp
from jax import lax
from jax.experimental import pallas as pl
from jax.experimental.pallas import tpu as pltpu
from jax.sharding import PartitionSpec as P

HEAD = 128
KV_HEADS = 4
GROUP = 8
LEN = 256
D = 8192
F32 = jnp.float32
BF16 = jnp.bfloat16
MESH = pl.DeviceIdType.MESH
N_X, N_Y, N_Z = 4, 4, 8
RA, RB, RC = 32, 32, 64
SLOTS = 192
ORDER = (
    "stat", "ga", "gb", "gc", "att", "att", "att", "att", "ga", "att",
    "att", "gb", "att", "stat", "gc", "att", "gb", "ga", "gc", "stat",
    "coef", "pass2a", "pass2b", "part0", "rb", "gb", "part1", "rc", "ga", "part2",
    "part3", "ra", "gc", "rc", "rb", "rd", "rd", "gb", "rc", "rb",
    "ga", "gb", "ra", "rb", "gb", "rd", "gc", "gb", "rb", "ga",
    "ga", "rc", "ra", "rb", "rd", "rc", "gc", "rd", "ra", "gc",
    "prod", "rb", "rc", "prod", "prod", "prod", "prod", "rd", "prod", "prod",
    "ra", "prod",
)


def _coords():
    cuts = lax.axis_index("cuts")
    fsdp = lax.axis_index("fsdp")
    core = cuts % 2
    y_hi = cuts // 2
    y_lo = fsdp // 32
    z = (fsdp // 4) % 8
    x = fsdp % 4
    return x, y_hi * 2 + y_lo, z, core


def _device(x, y, z, core):
    return ((y // 2) * 2 + core, (y % 2) * 32 + z * 4 + x)


def _nt(a, b):
    return lax.dot_general(a, b, (((1,), (1,)), ((), ())), preferred_element_type=F32)


def _nn(a, b):
    return lax.dot_general(a, b, (((1,), (0,)), ((), ())), preferred_element_type=F32)


def kernel(
    hid, w, q, k, og, nlp, olp, rew, rlen, gid,
    ig, wg, cf,
    hv, qv, ogv, kv, pt, douts, dvs, dvf, dvr, dvt, W,
    PA, PB, PC, rax, ray, raz, rcy, rcx, rcz, rbz, rbx, rby,
    fin, st, rsp, rsz, rsc, coefv,
    ssem, rsem, lsem, nlv, olv, rwv, rlv, giv,
):
    x, y, z, c = _coords()
    y_lo, y_hi = y % 2, y // 2

    def xs(d):
        return (x + d + N_X) % N_X

    def ys(d):
        return (y + d + N_Y) % N_Y

    def zs(d):
        return (z + d + N_Z) % N_Z

    def at_x(d):
        return _device(xs(d), y, z, c)

    def at_y(d):
        return _device(x, ys(d), z, c)

    def at_z(d):
        return _device(x, y, zs(d), c)

    partner = _device(x, y, z, 1 - c)
    sent = []

    def send(src, dst, device):
        i = len(sent)
        copy = pltpu.make_async_remote_copy(
            src_ref=src, dst_ref=dst, send_sem=ssem.at[i], recv_sem=rsem.at[i],
            device_id=device, device_id_type=MESH,
        )
        copy.start()
        sent.append(copy)
        return copy

    loads = [
        pltpu.make_async_copy(q, qv, lsem.at[0]),
        pltpu.make_async_copy(og, ogv, lsem.at[1]),
        pltpu.make_async_copy(hid, hv.at[pl.ds(0, LEN)], lsem.at[2]),
        pltpu.make_async_copy(k, kv, lsem.at[3]),
        pltpu.make_async_copy(
            w.at[pl.ds(pl.multiple_of(64 * c, 64), 64)], W.at[c, y_lo, z, x], lsem.at[4]
        ),
    ]
    for i, (src, dst) in enumerate(((nlp, nlv), (olp, olv), (rew, rwv), (rlen, rlv), (gid, giv))):
        loads.append(pltpu.make_async_copy(src, dst, lsem.at[5 + i]))
    for i in (5, 6, 7, 8, 9, 4, 3, 0, 1, 2):
        loads[i].start()

    barrier = pltpu.get_barrier_semaphore()
    around = [at_x(1), at_x(-1), at_x(2), at_y(1), at_y(-1), at_y(2), partner]
    around += [at_z(d) for d in range(1, 8)]
    around += [_device(x, ys(2), z, 1 - c)]
    flip = y_hi * 2 + (1 - y_lo)
    around += [_device(xs(d), flip, z, c) for d in range(1, 4)]
    for device in around:
        pl.semaphore_signal(barrier, inc=1, device_id=device, device_id_type=MESH)

    for load in loads[5:]:
        load.wait()
    lane = lax.broadcasted_iota(jnp.int32, (8, 128), 1)
    group = giv[...]
    reward = rwv[...]
    length = rlv[...].astype(F32)
    position = lax.broadcasted_iota(jnp.int32, (1, LEN), 1)
    live = (position < rlv[...]).astype(F32)
    ratio = jnp.exp(nlv[...] - olv[...])
    outside = jnp.logical_or(ratio > 1.28, ratio < 0.8).astype(F32)
    clipped = jnp.sum(live * outside, axis=1, keepdims=True)
    member = (lane % 8 == group).astype(F32)
    stats = jnp.where(
        lane < 8, member,
        jnp.where(
            lane < 16, member * reward,
            jnp.where(
                lane < 24, member * (reward * reward),
                jnp.where(lane == 24, length, jnp.where(lane == 25, clipped, 0.0)),
            ),
        ),
    )
    st[0] = stats
    pl.semaphore_wait(barrier, len(around))

    def stats_steps():
        copies = [send(st.at[0], rsz.at[d - 1], at_z(d)) for d in (4, 3, 5, 2, 6, 1, 7)]
        yield
        for copy in copies:
            copy.wait_recv()
        total = st[0]
        for i in range(7):
            total = total + rsz[i]
        st[1] = total
        plane = [(d, to) for d in (2, 1, 3) for to in (flip, y)] + [(0, flip)]
        copies = [send(st.at[1], rsp.at[i], _device(xs(d), to, z, c)) for i, (d, to) in enumerate(plane)]
        yield
        for copy in copies:
            copy.wait_recv()
        total = st[1]
        for i in range(7):
            total = total + rsp[i]
        st[3] = total
        copies = [
            send(st.at[3], rsc.at[0], at_y(2)),
            send(st.at[3], rsc.at[1], partner),
            send(st.at[3], rsc.at[2], _device(x, ys(2), z, 1 - c)),
        ]
        yield
        for copy in copies:
            copy.wait_recv()
        every = ((st[3] + rsc[0]) + (rsc[1] + rsc[2]))[0:1]
        top = lane[0:1]
        all_live = jnp.sum(jnp.where(top == 24, every, 0.0), axis=1, keepdims=True)
        all_out = jnp.sum(jnp.where(top == 25, every, 0.0), axis=1, keepdims=True)
        cf[...] = all_out / all_live

    def ring_z(view, half):
        up = send(view(z), view(z), at_z(1))
        down = send(view(z), view(z), at_z(-1))
        yield
        for d in (1, 2, 3):
            up.wait_recv()
            down.wait_recv()
            if d < 3:
                up = send(view(zs(-d)), view(zs(-d)), at_z(1))
                down = send(view(zs(d)), view(zs(d)), at_z(-1))
            else:
                up = send(half(zs(-3), 0), half(zs(-3), 0), at_z(1))
                down = send(half(zs(3), 1), half(zs(3), 1), at_z(-1))
            yield
        up.wait_recv()
        down.wait_recv()

    def near_z(view, half):
        copies = [send(view(z), view(z), at_z(d)) for d in (2, -2, 1, -1)]
        yield
        for copy in copies:
            copy.wait_recv()
        below, above = zs(-2), zs(2)
        copies = [
            send(half(below, 0), half(below, 0), at_z(2)),
            send(half(above, 1), half(above, 1), at_z(-2)),
            send(view(below), view(below), at_z(1)),
            send(view(above), view(above), at_z(-1)),
        ]
        yield
        for copy in copies:
            copy.wait_recv()

    forwards = []

    def gather_a():
        own = W.at[c, y_lo, z, x, pl.ds(0, 16)]
        copy = send(own, own, at_y(1))
        yield
        copy.wait_recv()
        yield from near_z(
            lambda i: W.at[c, :, i, x, pl.ds(0, 16)],
            lambda i, h: W.at[c, h, i, x, pl.ds(0, 16)],
        )

        def view(i):
            return W.at[c, :, :, i, pl.ds(0, 16)]

        def half(i, h):
            return W.at[c, h, :, i, pl.ds(0, 16)]

        up = send(view(x), view(x), at_x(1))
        down = send(view(x), view(x), at_x(-1))
        forwards.append(send(view(x), view(x), partner))
        yield
        up.wait_recv()
        down.wait_recv()
        up = send(half(xs(-1), 0), half(xs(-1), 0), at_x(1))
        down = send(half(xs(1), 1), half(xs(1), 1), at_x(-1))
        forwards.append(send(view(xs(-1)), view(xs(-1)), partner))
        forwards.append(send(view(xs(1)), view(xs(1)), partner))
        yield
        up.wait_recv()
        down.wait_recv()
        forwards.append(send(view(xs(2)), view(xs(2)), partner))

    def gather_b():
        own = W.at[c, y_lo, z, x, pl.ds(16, 16)]
        copies = [send(own, own, at_x(d)) for d in (1, 2, 3)]
        yield
        for copy in copies:
            copy.wait_recv()
        left = W.at[c, y_lo, z, pl.ds(0, 2), pl.ds(16, 16)]
        right = W.at[c, y_lo, z, pl.ds(2, 2), pl.ds(16, 16)]
        copies = [send(left, left, at_y(1)), send(right, right, at_y(-1))]
        yield
        for copy in copies:
            copy.wait_recv()
        def view(i):
            return W.at[c, :, i, :, pl.ds(16, 16)]

        yield from ring_z(view, lambda i, h: W.at[c, h, i, :, pl.ds(16, 16)])
        whole = W.at[c, :, :, :, pl.ds(16, 16)]
        forwards.append(send(whole, whole, partner))

    def gather_c():
        yield from near_z(
            lambda i: W.at[c, y_lo, i, x, pl.ds(32, 32)],
            lambda i, h: W.at[c, y_lo, i, x, pl.ds(32 + 16 * h, 16)],
        )
        final = []

        def view(i):
            return W.at[c, y_lo, :, i, pl.ds(32, 32)]

        def half(i, h):
            return W.at[c, y_lo, pl.ds(4 * h, 4), i, pl.ds(32, 32)]

        def across(i):
            final.append(send(half(i, 0), half(i, 0), at_y(1)))
            final.append(send(half(i, 1), half(i, 1), at_y(-1)))

        up = send(view(x), view(x), at_x(1))
        down = send(view(x), view(x), at_x(-1))
        across(x)
        yield
        up.wait_recv()
        down.wait_recv()
        up = send(half(xs(-1), 0), half(xs(-1), 0), at_x(1))
        down = send(half(xs(1), 1), half(xs(1), 1), at_x(-1))
        across(xs(-1))
        across(xs(1))
        yield
        up.wait_recv()
        down.wait_recv()
        across(xs(2))
        mine = W.at[c, y_lo, :, :, pl.ds(32, 32)]
        forwards.append(send(mine, mine, partner))
        yield
        for copy in final:
            copy.wait_recv()
        theirs = W.at[c, 1 - y_lo, :, :, pl.ds(32, 32)]
        forwards.append(send(theirs, theirs, partner))

    done = []

    def advance(steps):
        for step in steps:
            if step not in done and next(step, "end") == "end":
                done.append(step)

    def left(*lists):
        return any(step not in done for steps in lists for step in steps)

    factor = (1.0 / HEAD**0.5) * 1.4426950408889634
    row = lax.broadcasted_iota(jnp.int32, (HEAD, HEAD), 0)
    col = lax.broadcasted_iota(jnp.int32, (HEAD, HEAD), 1)
    causal = row <= col

    def soft(scores):
        top = jnp.max(scores, axis=0, keepdims=True)
        expo = jnp.exp2((scores - top) * factor)
        return (expo * (1.0 / jnp.sum(expo, axis=0, keepdims=True))).astype(BF16)

    def attend(head, first):
        keys = kv[:, head * HEAD:(head + 1) * HEAD]

        def one(i, carry):
            g = first + i
            n = head * GROUP + g
            query = qv[:, pl.ds(pl.multiple_of(n * HEAD, HEAD), HEAD)]
            early = jnp.where(causal, _nt(keys[:128], query[:128]), -1e30)
            late = _nt(keys, query[128:])
            late = jnp.concatenate([late[:128], jnp.where(causal, late[128:], -1e30)], axis=0)
            at = pl.multiple_of(g * LEN, LEN)
            pt[head, pl.ds(0, 128), pl.ds(at, 128)] = soft(early)
            pt[head, pl.ds(128, 128), pl.ds(at, 128)] = jnp.zeros((128, 128), BF16)
            pt[head, :, pl.ds(at + 128, 128)] = soft(late)
            return carry

        lax.fori_loop(0, 4, one, 0)

    attended = []

    def attend_next():
        if not attended:
            loads[3].wait()
            loads[0].wait()
        attend(len(attended) // 2, 4 * (len(attended) % 2))
        attended.append(0)

    def make_coef():
        slice_total = st[3][0:1]
        top = lane[0:1]

        def pick(at):
            return jnp.sum(jnp.where(top == at, slice_total, 0.0), axis=1, keepdims=True)

        own_cnt, own_one, own_two = pick(group), pick(8 + group), pick(16 + group)
        mean = own_one / own_cnt
        var = own_two / own_cnt - mean * mean
        adv = (reward - mean) / jnp.sqrt(var + 0.25)
        total = pick(24) * 4.0
        active = jnp.where(adv > 0, (ratio < 1.28).astype(F32), (ratio > 0.8).astype(F32))
        coef = -live * adv * ratio * active * (65536.0 / total)
        square = (LEN, LEN)
        diagonal = lax.broadcasted_iota(jnp.int32, square, 0) == lax.broadcasted_iota(jnp.int32, square, 1)
        coefv[...] = jnp.broadcast_to(
            jnp.sum(jnp.where(diagonal, coef, 0.0), axis=1, keepdims=True), (LEN, HEAD)
        )
        loads[1].wait()

    def dvalue(core):
        for i in range(2):
            head = 2 * core + i
            for g in range(GROUP):
                columns = pl.ds(pl.multiple_of((head * GROUP + g) * HEAD, HEAD), HEAD)
                douts[g * LEN:(g + 1) * LEN, :] = (coefv[...] * ogv[:, columns].astype(F32)).astype(BF16)
            piece = _nn(pt[head], douts[...]).astype(BF16)
            dvs[core, :, i * HEAD:(i + 1) * HEAD] = piece
            dvf[:, pl.ds(pl.multiple_of(head * HEAD, HEAD), HEAD)] = piece

    dv_copies = []

    def dvalue_other():
        dvalue(1 - c)
        dv_copies.append(send(dvs.at[1 - c], dvr, partner))

    def dvalue_own():
        dvalue(c)
        dvt[:, 0:LEN] = dvs[c].T

    def meet():
        dv_copies[0].wait_recv()
        dvt[:, LEN:2 * LEN] = dvr[...].T
        loads[2].wait()
        hidden_copy.wait_recv()

    def partial(yl, first, count):
        def one(i, carry):
            zz = zs(first + i)
            columns = pl.ds(pl.multiple_of((yl * 8 + zz) * 512, 512), 512)
            block = _nn(dvt[...], hv[:, columns]).astype(BF16)
            for i in range(N_X):
                b = block[:, i * 128:(i + 1) * 128]
                PA[yl, zz, i, 0] = b[0:32]
                PA[yl, zz, i, 1] = b[32:64]
                PB[yl, zz, i, 0] = b[64:96]
                PB[yl, zz, i, 1] = b[96:128]
                PC[yl, zz, i, 0] = b[128:192]
                PC[yl, zz, i, 1] = b[192:256]
            return carry

        lax.fori_loop(0, count, one, 0)

    def added(*terms):
        total = terms[0].astype(F32)
        for term in terms[1:]:
            total = total + term.astype(F32)
        return total

    def reduce_a(first, size):
        part = pl.ds(first, size)
        up = send(PA.at[:, :, xs(2), 0, part], rax.at[0, :, :, part], at_x(1))
        down = send(PA.at[:, :, xs(2), 1, part], rax.at[1, :, :, part], at_x(-1))
        up_b = send(PA.at[:, :, xs(1), 1, part], rax.at[2, :, :, part], at_x(1))
        down_b = send(PA.at[:, :, xs(-1), 0, part], rax.at[3, :, :, part], at_x(-1))
        yield
        up.wait_recv()
        PA[:, :, xs(1), 0, part] = added(PA[:, :, xs(1), 0, part], rax[0, :, :, part]).astype(BF16)
        up = send(PA.at[:, :, xs(1), 0, part], rax.at[4, :, :, part], at_x(1))
        down.wait_recv()
        PA[:, :, xs(-1), 1, part] = added(PA[:, :, xs(-1), 1, part], rax[1, :, :, part]).astype(BF16)
        down = send(PA.at[:, :, xs(-1), 1, part], rax.at[5, :, :, part], at_x(-1))
        yield
        up_b.wait_recv()
        down_b.wait_recv()
        up.wait_recv()
        down.wait_recv()
        PA[:, :, x, 0, part] = added(PA[:, :, x, 0, part], rax[3, :, :, part], rax[4, :, :, part]).astype(BF16)
        PA[:, :, x, 1, part] = added(PA[:, :, x, 1, part], rax[2, :, :, part], rax[5, :, :, part]).astype(BF16)
        copies = [send(PA.at[ys(d) % 2, :, x, ys(d) // 2, part], ray.at[d - 1, :, part], at_y(d)) for d in (2, 1, 3)]
        yield
        for copy in copies:
            copy.wait_recv()
        PA[y_lo, :, x, y_hi, part] = added(PA[y_lo, :, x, y_hi, part], ray[0, :, part], ray[1, :, part], ray[2, :, part]).astype(BF16)
        copies = [send(PA.at[y_lo, zs(d), x, y_hi, part], raz.at[d - 1, part], at_z(d)) for d in (4, 3, 5, 2, 6, 1, 7)]
        yield
        for copy in copies:
            copy.wait_recv()
        fin[y_hi, c, part] = added(PA[y_lo, z, x, y_hi, part], *[raz[i, part] for i in range(7)]).astype(BF16)

    def reduce_c(first, size):
        part = pl.ds(first, size)

        def view(d, h):
            return PC.at[ys(d) % 2, pl.ds(4 * h, 4), :, ys(d) // 2, part]

        def get(d, h):
            return PC[ys(d) % 2, pl.ds(4 * h, 4), :, ys(d) // 2, part]

        def put(d, h, value):
            PC[ys(d) % 2, pl.ds(4 * h, 4), :, ys(d) // 2, part] = value.astype(BF16)

        up = send(view(2, 0), rcy.at[0, :, :, part], at_y(1))
        down = send(view(2, 1), rcy.at[1, :, :, part], at_y(-1))
        yield
        up_b = send(view(1, 1), rcy.at[2, :, :, part], at_y(1))
        down_b = send(view(-1, 0), rcy.at[3, :, :, part], at_y(-1))
        yield
        up.wait_recv()
        put(1, 0, added(get(1, 0), rcy[0, :, :, part]))
        up = send(view(1, 0), rcy.at[4, :, :, part], at_y(1))
        down.wait_recv()
        put(-1, 1, added(get(-1, 1), rcy[1, :, :, part]))
        down = send(view(-1, 1), rcy.at[5, :, :, part], at_y(-1))
        yield
        up_b.wait_recv()
        down_b.wait_recv()
        up.wait_recv()
        down.wait_recv()
        put(0, 0, added(get(0, 0), rcy[3, :, :, part], rcy[4, :, :, part]))
        put(0, 1, added(get(0, 1), rcy[2, :, :, part], rcy[5, :, :, part]))
        copies = [send(PC.at[y_lo, :, xs(d), y_hi, part], rcx.at[d - 1, :, part], at_x(d)) for d in (2, 1, 3)]
        yield
        for copy in copies:
            copy.wait_recv()
        PC[y_lo, :, x, y_hi, part] = added(PC[y_lo, :, x, y_hi, part], rcx[0, :, part], rcx[1, :, part], rcx[2, :, part]).astype(BF16)
        copies = [send(PC.at[y_lo, zs(d), x, y_hi, part], rcz.at[d - 1, part], at_z(d)) for d in (4, 3, 5, 2, 6, 1, 7)]
        yield
        for copy in copies:
            copy.wait_recv()
        fin[y_hi, c, pl.ds(RA + RB + first, size)] = added(
            PC[y_lo, z, x, y_hi, part], *[rcz[i, part] for i in range(7)]
        ).astype(BF16)

    def reduce_b(first, size):
        part = pl.ds(first, size)
        up = send(PB.at[:, zs(4), :, 0, part], rbz.at[0, :, :, 0, part], at_z(1))
        down = send(PB.at[:, zs(4), :, 1, part], rbz.at[0, :, :, 1, part], at_z(-1))
        yield
        up.wait_recv()
        PB[:, zs(3), :, 0, part] = added(PB[:, zs(3), :, 0, part], rbz[0, :, :, 0, part]).astype(BF16)
        up = send(PB.at[:, zs(3), :, :, part], rbz.at[1, :, :, :, part], at_z(1))
        down.wait_recv()
        PB[:, zs(-3), :, 1, part] = added(PB[:, zs(-3), :, 1, part], rbz[0, :, :, 1, part]).astype(BF16)
        down = send(PB.at[:, zs(-3), :, :, part], rbz.at[2, :, :, :, part], at_z(-1))
        yield
        for d in (2, 1):
            up.wait_recv()
            PB[:, zs(d), :, :, part] = added(PB[:, zs(d), :, :, part], rbz[5 - 2 * d, :, :, :, part]).astype(BF16)
            up = send(PB.at[:, zs(d), :, :, part], rbz.at[7 - 2 * d, :, :, :, part], at_z(1))
            down.wait_recv()
            PB[:, zs(-d), :, :, part] = added(PB[:, zs(-d), :, :, part], rbz[6 - 2 * d, :, :, :, part]).astype(BF16)
            down = send(PB.at[:, zs(-d), :, :, part], rbz.at[8 - 2 * d, :, :, :, part], at_z(-1))
            yield
        up.wait_recv()
        down.wait_recv()
        PB[:, z, :, :, part] = added(PB[:, z, :, :, part], rbz[5, :, :, :, part], rbz[6, :, :, :, part]).astype(BF16)
        copies = [send(PB.at[:, z, xs(d), :, part], rbx.at[d - 1, :, :, part], at_x(d)) for d in (2, 1, 3)]
        yield
        for copy in copies:
            copy.wait_recv()
        PB[:, z, x, :, part] = added(PB[:, z, x, :, part], rbx[0, :, :, part], rbx[1, :, :, part], rbx[2, :, :, part]).astype(BF16)
        copies = [send(PB.at[ys(d) % 2, z, x, ys(d) // 2, part], rby.at[d - 1, part], at_y(d)) for d in (2, 1, 3)]
        yield
        for copy in copies:
            copy.wait_recv()
        fin[y_hi, c, pl.ds(RA + first, size)] = added(PB[y_lo, z, x, y_hi, part], rby[0, part], rby[1, part], rby[2, part]).astype(BF16)

    def product(t, carry):
        yl, zz = t // 8, t % 8
        rows = jnp.concatenate([W[h, yl, zz, i] for i in range(N_X) for h in range(2)], axis=0)
        ig[:, pl.ds(pl.multiple_of(t * 512, 512), 512)] = _nt(dvf[...], rows).astype(BF16)
        return carry

    products = []

    def product_next():
        if not products:
            for copy in forwards:
                copy.wait_recv()
        first = 2 * len(products)
        lax.fori_loop(first, first + 2, product, 0)
        products.append(0)

    steps = {
        "stat": stats_steps(),
        "ga": gather_a(),
        "gb": gather_b(),
        "gc": gather_c(),
        "ra": reduce_a(0, RA),
        "rb": reduce_b(0, RB),
        "rc": reduce_c(0, 32),
        "rd": reduce_c(32, 32),
    }

    def partial_first():
        meet()
        partial(y_lo, 4, 1)
        partial(1 - y_lo, 4, 1)

    def partial_third():
        partial(1 - y_lo, 3, 1)
        partial(1 - y_lo, 5, 1)

    work = {
        "att": attend_next,
        "coef": make_coef,
        "pass2a": dvalue_other,
        "pass2b": dvalue_own,
        "part0": partial_first,
        "part1": lambda: partial(y_lo, 5, 7),
        "part2": partial_third,
        "part3": lambda: partial(1 - y_lo, 6, 5),
        "prod": product_next,
    }
    hidden_copy = send(hid, hv.at[pl.ds(LEN, LEN)], partner)
    loads[4].wait()
    for name in ORDER:
        if name in work:
            work[name]()
        else:
            advance([steps[name]])
    advance(list(steps.values()))
    while left(steps.values()):
        advance(list(steps.values()))

    mine = fin.at[y_hi, c]
    copies = [
        send(mine, mine, at_y(2)),
        send(mine, mine, partner),
        send(mine, mine, _device(x, ys(2), z, 1 - c)),
    ]
    for copy in copies:
        copy.wait_recv()
    pieces = []
    for core in range(2):
        for first, size in ((0, RA), (RA, RB), (RA + RB, RC)):
            for half in range(2):
                pieces.append(fin[half, core, pl.ds(first, size)])
    wg[...] = jnp.concatenate(pieces, axis=0).astype(F32).T

    for copy in sent:
        copy.wait_send()


def write_out(ig, wg, ig_out, wg_out, sem):
    rows = LEN // 8
    copies = [pltpu.make_async_copy(wg, wg_out, sem.at[8])]
    for i in range(8):
        part = pl.ds(i * rows, rows)
        copies.append(pltpu.make_async_copy(ig.at[part], ig_out.at[part], sem.at[i]))
    for copy in copies:
        copy.start()
    for copy in copies:
        copy.wait()


def local(
    hidden_in, value_weight, queries, keys, out_grad, new_logp, old_logp, rewards, resp_len, group_id
):
    vmem = pl.BlockSpec(memory_space=pltpu.VMEM)
    hbm = pl.BlockSpec(memory_space=pltpu.HBM)
    bf = functools.partial(pltpu.VMEM, dtype=BF16)
    scratch = [
        bf((2 * LEN, D)),
        bf((LEN, 4096)),
        bf((LEN, 4096)),
        bf((LEN, 512)),
        bf((KV_HEADS, LEN, GROUP * LEN)),
        bf((GROUP * LEN, HEAD)),
        bf((2, LEN, 256)),
        bf((LEN, 512)),
        bf((LEN, 256)),
        bf((256, 2 * LEN)),
        bf((2, 2, 8, 4, 64, 512)),
        bf((2, 8, 4, 2, RA, 128)),
        bf((2, 8, 4, 2, RB, 128)),
        bf((2, 8, 4, 2, RC, 128)),
        bf((6, 2, 8, RA, 128)),
        bf((3, 8, RA, 128)),
        bf((7, RA, 128)),
        bf((6, 4, 4, RC, 128)),
        bf((3, 8, RC, 128)),
        bf((7, RC, 128)),
        bf((7, 2, 4, 2, RB, 128)),
        bf((3, 2, 2, RB, 128)),
        bf((3, RB, 128)),
        bf((2, 2, 128, 128)),
        pltpu.VMEM((4, 8, 128), F32),
        pltpu.VMEM((7, 8, 128), F32),
        pltpu.VMEM((7, 8, 128), F32),
        pltpu.VMEM((3, 8, 128), F32),
        pltpu.VMEM((LEN, HEAD), F32),
        pltpu.SemaphoreType.DMA((SLOTS,)),
        pltpu.SemaphoreType.DMA((SLOTS,)),
        pltpu.SemaphoreType.DMA((10,)),
        pltpu.VMEM((1, LEN), F32),
        pltpu.VMEM((1, LEN), F32),
        pltpu.VMEM((1, 1), F32),
        pltpu.VMEM((1, 1), jnp.int32),
        pltpu.VMEM((1, 1), jnp.int32),
    ]
    input_grad, weight_grad, clip_frac = pl.pallas_call(
        kernel,
        out_shape=(
            pltpu.VMEM((LEN, D), BF16),
            pltpu.VMEM((128, 512), F32),
            jax.ShapeDtypeStruct((1, 1), F32),
        ),
        in_specs=[hbm] * 10,
        out_specs=(vmem, vmem, vmem),
        scratch_shapes=scratch,
        compiler_params=pltpu.CompilerParams(
            collective_id=0, has_side_effects=True, vmem_limit_bytes=56 << 20
        ),
        name="value_backward",
    )(
        hidden_in, value_weight, queries, keys, out_grad,
        new_logp.reshape(1, LEN), old_logp.reshape(1, LEN), rewards.reshape(1, 1), resp_len, group_id,
    )
    input_grad, weight_grad = pl.pallas_call(
        write_out,
        out_shape=(
            jax.ShapeDtypeStruct((LEN, D), BF16),
            jax.ShapeDtypeStruct((128, 512), F32),
        ),
        in_specs=[vmem, vmem],
        out_specs=(hbm, hbm),
        scratch_shapes=[pltpu.SemaphoreType.DMA((9,))],
        compiler_params=pltpu.CompilerParams(vmem_limit_bytes=4 << 20),
        name="write_out",
    )(input_grad, weight_grad)
    return input_grad, weight_grad, clip_frac.reshape(())


def solution(mesh):
    rows = P(("cuts", "fsdp"), None)
    flat = P(("cuts", "fsdp"))
    return jax.shard_map(
        local,
        mesh=mesh,
        in_specs=(
            rows, P("fsdp", None), rows, rows, rows, flat, flat, flat, P("cuts", "fsdp"), P("cuts", "fsdp"),
        ),
        out_specs=(rows, P("fsdp", None), P()),
        check_vma=False,
    )
```

```python
import functools

import jax
import jax.numpy as jnp
from jax import lax
from jax.experimental import pallas as pl
from jax.experimental.pallas import tpu as pltpu
from jax.sharding import PartitionSpec as P

HEAD = 128
KV_HEADS = 4
GROUP = 8
LEN = 256
D = 8192
F32 = jnp.float32
BF16 = jnp.bfloat16
MESH = pl.DeviceIdType.MESH
N_X, N_Y, N_Z = 4, 4, 8
RA, RB, RC = 32, 32, 64
SLOTS = 192
ORDER = (
    "stat", "ga", "gb", "gc", "att", "att", "att", "att", "ga", "att",
    "att", "gb", "att", "stat", "gc", "att", "gb", "ga", "gc", "stat",
    "coef", "pass2a", "pass2b", "part0", "rb", "gb", "part1", "rc", "ga", "part2",
    "part3", "ra", "gc", "rc", "rb", "rd", "rd", "gb", "rc", "rb",
    "ga", "gb", "ra", "rb", "gb", "rd", "gc", "gc", "gc", "rb",
    "ga", "prod", "prod", "prod", "ra", "rc", "prod", "rb", "prod", "rd",
    "prod", "gc", "rc", "prod", "prod", "ra", "rd", "rb", "rc", "ra",
    "rd",
)


def _coords():
    cuts = lax.axis_index("cuts")
    fsdp = lax.axis_index("fsdp")
    core = cuts % 2
    y_hi = cuts // 2
    y_lo = fsdp // 32
    z = (fsdp // 4) % 8
    x = fsdp % 4
    return x, y_hi * 2 + y_lo, z, core


def _device(x, y, z, core):
    return ((y // 2) * 2 + core, (y % 2) * 32 + z * 4 + x)


def _nt(a, b):
    return lax.dot_general(a, b, (((1,), (1,)), ((), ())), preferred_element_type=F32)


def _nn(a, b):
    return lax.dot_general(a, b, (((1,), (0,)), ((), ())), preferred_element_type=F32)


def kernel(
    hid, w, q, k, og, nlp, olp, rew, rlen, gid,
    ig, wg, cf,
    hv, qv, ogv, kv, pt, douts, dvs, dvf, dvr, dvt, W,
    PA, PB, PC, rax, ray, raz, rcy, rcx, rcz, rbz, rbx, rby,
    fin, st, rsp, rsz, rsc, coefv,
    ssem, rsem, lsem, nlv, olv, rwv, rlv, giv,
):
    x, y, z, c = _coords()
    y_lo, y_hi = y % 2, y // 2

    def xs(d):
        return (x + d + N_X) % N_X

    def ys(d):
        return (y + d + N_Y) % N_Y

    def zs(d):
        return (z + d + N_Z) % N_Z

    def at_x(d):
        return _device(xs(d), y, z, c)

    def at_y(d):
        return _device(x, ys(d), z, c)

    def at_z(d):
        return _device(x, y, zs(d), c)

    partner = _device(x, y, z, 1 - c)
    sent = []

    def send(src, dst, device):
        i = len(sent)
        copy = pltpu.make_async_remote_copy(
            src_ref=src, dst_ref=dst, send_sem=ssem.at[i], recv_sem=rsem.at[i],
            device_id=device, device_id_type=MESH,
        )
        copy.start()
        sent.append(copy)
        return copy

    loads = [
        pltpu.make_async_copy(q, qv, lsem.at[0]),
        pltpu.make_async_copy(og, ogv, lsem.at[1]),
        pltpu.make_async_copy(hid, hv.at[pl.ds(0, LEN)], lsem.at[2]),
        pltpu.make_async_copy(k, kv, lsem.at[3]),
        pltpu.make_async_copy(
            w.at[pl.ds(pl.multiple_of(64 * c, 64), 64)], W.at[c, y_lo, z, x], lsem.at[4]
        ),
    ]
    for i, (src, dst) in enumerate(((nlp, nlv), (olp, olv), (rew, rwv), (rlen, rlv), (gid, giv))):
        loads.append(pltpu.make_async_copy(src, dst, lsem.at[5 + i]))
    for i in (5, 6, 7, 8, 9, 4, 3, 0, 1, 2):
        loads[i].start()

    barrier = pltpu.get_barrier_semaphore()
    around = [at_x(1), at_x(-1), at_x(2), at_y(1), at_y(-1), at_y(2), partner]
    around += [at_z(d) for d in range(1, 8)]
    around += [_device(x, ys(2), z, 1 - c)]
    flip = y_hi * 2 + (1 - y_lo)
    around += [_device(xs(d), flip, z, c) for d in range(1, 4)]
    for device in around:
        pl.semaphore_signal(barrier, inc=1, device_id=device, device_id_type=MESH)

    for load in loads[5:]:
        load.wait()
    lane = lax.broadcasted_iota(jnp.int32, (8, 128), 1)
    group = giv[...]
    reward = rwv[...]
    length = rlv[...].astype(F32)
    position = lax.broadcasted_iota(jnp.int32, (1, LEN), 1)
    live = (position < rlv[...]).astype(F32)
    ratio = jnp.exp(nlv[...] - olv[...])
    outside = jnp.logical_or(ratio > 1.28, ratio < 0.8).astype(F32)
    clipped = jnp.sum(live * outside, axis=1, keepdims=True)
    member = (lane % 8 == group).astype(F32)
    stats = jnp.where(
        lane < 8, member,
        jnp.where(
            lane < 16, member * reward,
            jnp.where(
                lane < 24, member * (reward * reward),
                jnp.where(lane == 24, length, jnp.where(lane == 25, clipped, 0.0)),
            ),
        ),
    )
    st[0] = stats
    pl.semaphore_wait(barrier, len(around))

    def stats_steps():
        copies = [send(st.at[0], rsz.at[d - 1], at_z(d)) for d in (4, 3, 5, 2, 6, 1, 7)]
        yield
        for copy in copies:
            copy.wait_recv()
        total = st[0]
        for i in range(7):
            total = total + rsz[i]
        st[1] = total
        plane = [(d, to) for d in (2, 1, 3) for to in (flip, y)] + [(0, flip)]
        copies = [send(st.at[1], rsp.at[i], _device(xs(d), to, z, c)) for i, (d, to) in enumerate(plane)]
        yield
        for copy in copies:
            copy.wait_recv()
        total = st[1]
        for i in range(7):
            total = total + rsp[i]
        st[3] = total
        copies = [
            send(st.at[3], rsc.at[0], at_y(2)),
            send(st.at[3], rsc.at[1], partner),
            send(st.at[3], rsc.at[2], _device(x, ys(2), z, 1 - c)),
        ]
        yield
        for copy in copies:
            copy.wait_recv()
        every = ((st[3] + rsc[0]) + (rsc[1] + rsc[2]))[0:1]
        top = lane[0:1]
        all_live = jnp.sum(jnp.where(top == 24, every, 0.0), axis=1, keepdims=True)
        all_out = jnp.sum(jnp.where(top == 25, every, 0.0), axis=1, keepdims=True)
        cf[...] = jnp.broadcast_to(all_out / all_live, (1, 128))

    def ring_z(view, half):
        up = send(view(z), view(z), at_z(1))
        down = send(view(z), view(z), at_z(-1))
        yield
        for d in (1, 2, 3):
            up.wait_recv()
            down.wait_recv()
            if d < 3:
                up = send(view(zs(-d)), view(zs(-d)), at_z(1))
                down = send(view(zs(d)), view(zs(d)), at_z(-1))
            else:
                up = send(half(zs(-3), 0), half(zs(-3), 0), at_z(1))
                down = send(half(zs(3), 1), half(zs(3), 1), at_z(-1))
            yield
        up.wait_recv()
        down.wait_recv()

    def near_z(view, half):
        copies = [send(view(z), view(z), at_z(d)) for d in (2, -2, 1, -1)]
        yield
        for copy in copies:
            copy.wait_recv()
        below, above = zs(-2), zs(2)
        copies = [
            send(half(below, 0), half(below, 0), at_z(2)),
            send(half(above, 1), half(above, 1), at_z(-2)),
            send(view(below), view(below), at_z(1)),
            send(view(above), view(above), at_z(-1)),
        ]
        yield
        for copy in copies:
            copy.wait_recv()

    forwards = {}

    def forward(key, ref):
        forwards.setdefault(key, []).append(send(ref, ref, partner))

    def gather_a():
        own = W.at[c, y_lo, z, x, pl.ds(0, 16)]
        copy = send(own, own, at_y(1))
        yield
        copy.wait_recv()
        yield from near_z(
            lambda i: W.at[c, :, i, x, pl.ds(0, 16)],
            lambda i, h: W.at[c, h, i, x, pl.ds(0, 16)],
        )

        def view(i):
            return W.at[c, :, :, i, pl.ds(0, 16)]

        def half(i, h):
            return W.at[c, h, :, i, pl.ds(0, 16)]

        up = send(view(x), view(x), at_x(1))
        down = send(view(x), view(x), at_x(-1))
        forward("A0", view(x))
        yield
        up.wait_recv()
        down.wait_recv()
        up = send(half(xs(-1), 0), half(xs(-1), 0), at_x(1))
        down = send(half(xs(1), 1), half(xs(1), 1), at_x(-1))
        forward("A1", view(xs(-1)))
        forward("A1", view(xs(1)))
        yield
        up.wait_recv()
        down.wait_recv()
        forward("A2", view(xs(2)))

    def gather_b():
        own = W.at[c, y_lo, z, x, pl.ds(16, 16)]
        copies = [send(own, own, at_x(d)) for d in (1, 2, 3)]
        yield
        for copy in copies:
            copy.wait_recv()
        left = W.at[c, y_lo, z, pl.ds(0, 2), pl.ds(16, 16)]
        right = W.at[c, y_lo, z, pl.ds(2, 2), pl.ds(16, 16)]
        copies = [send(left, left, at_y(1)), send(right, right, at_y(-1))]
        yield
        for copy in copies:
            copy.wait_recv()
        def view(i):
            return W.at[c, :, i, :, pl.ds(16, 16)]

        yield from ring_z(view, lambda i, h: W.at[c, h, i, :, pl.ds(16, 16)])
        whole = W.at[c, :, :, :, pl.ds(16, 16)]
        forward("B", whole)

    def gather_c():
        yield from near_z(
            lambda i: W.at[c, y_lo, i, x, pl.ds(32, 32)],
            lambda i, h: W.at[c, y_lo, i, x, pl.ds(32 + 16 * h, 16)],
        )
        final = []

        def view(i):
            return W.at[c, y_lo, :, i, pl.ds(32, 32)]

        def half(i, h):
            return W.at[c, y_lo, pl.ds(4 * h, 4), i, pl.ds(32, 32)]

        def across(i):
            final.append(send(half(i, 0), half(i, 0), at_y(1)))
            final.append(send(half(i, 1), half(i, 1), at_y(-1)))

        up = send(view(x), view(x), at_x(1))
        down = send(view(x), view(x), at_x(-1))
        across(x)
        yield
        up.wait_recv()
        down.wait_recv()
        up = send(half(xs(-1), 0), half(xs(-1), 0), at_x(1))
        down = send(half(xs(1), 1), half(xs(1), 1), at_x(-1))
        across(xs(-1))
        across(xs(1))
        yield
        up.wait_recv()
        down.wait_recv()
        across(xs(2))
        forward("M", W.at[c, y_lo, :, :, pl.ds(32, 32)])
        yield
        for key, copies, places in (
            ("C0", final[0:2], (x,)),
            ("C1", final[2:6], (xs(-1), xs(1))),
            ("C2", final[6:8], (xs(2),)),
        ):
            for copy in copies:
                copy.wait_recv()
            for i in places:
                forward(key, W.at[c, 1 - y_lo, :, i, pl.ds(32, 32)])
            yield

    done = []

    def advance(steps):
        for step in steps:
            if step not in done and next(step, "end") == "end":
                done.append(step)

    def left(*lists):
        return any(step not in done for steps in lists for step in steps)

    factor = (1.0 / HEAD**0.5) * 1.4426950408889634
    row = lax.broadcasted_iota(jnp.int32, (HEAD, HEAD), 0)
    col = lax.broadcasted_iota(jnp.int32, (HEAD, HEAD), 1)
    causal = row <= col

    def soft(scores):
        top = jnp.max(scores, axis=0, keepdims=True)
        expo = jnp.exp2((scores - top) * factor)
        return (expo * (1.0 / jnp.sum(expo, axis=0, keepdims=True))).astype(BF16)

    def attend(head, first):
        keys = kv[:, head * HEAD:(head + 1) * HEAD]

        def one(i, carry):
            g = first + i
            n = head * GROUP + g
            query = qv[:, pl.ds(pl.multiple_of(n * HEAD, HEAD), HEAD)]
            early = jnp.where(causal, _nt(keys[:128], query[:128]), -1e30)
            late = _nt(keys, query[128:])
            late = jnp.concatenate([late[:128], jnp.where(causal, late[128:], -1e30)], axis=0)
            at = pl.multiple_of(g * LEN, LEN)
            pt[head, pl.ds(0, 128), pl.ds(at, 128)] = soft(early)
            pt[head, pl.ds(128, 128), pl.ds(at, 128)] = jnp.zeros((128, 128), BF16)
            pt[head, :, pl.ds(at + 128, 128)] = soft(late)
            return carry

        lax.fori_loop(0, 4, one, 0, unroll=2)

    attended = []

    def attend_next():
        if not attended:
            loads[3].wait()
            loads[0].wait()
        attend(len(attended) // 2, 4 * (len(attended) % 2))
        attended.append(0)

    def make_coef():
        slice_total = st[3][0:1]
        top = lane[0:1]

        def pick(at):
            return jnp.sum(jnp.where(top == at, slice_total, 0.0), axis=1, keepdims=True)

        own_cnt, own_one, own_two = pick(group), pick(8 + group), pick(16 + group)
        mean = own_one / own_cnt
        var = own_two / own_cnt - mean * mean
        adv = (reward - mean) / jnp.sqrt(var + 0.25)
        total = pick(24) * 4.0
        active = jnp.where(adv > 0, (ratio < 1.28).astype(F32), (ratio > 0.8).astype(F32))
        coef = -live * adv * ratio * active * (65536.0 / total)
        square = (LEN, LEN)
        diagonal = lax.broadcasted_iota(jnp.int32, square, 0) == lax.broadcasted_iota(jnp.int32, square, 1)
        coefv[...] = jnp.broadcast_to(
            jnp.sum(jnp.where(diagonal, coef, 0.0), axis=1, keepdims=True), (LEN, HEAD)
        )
        loads[1].wait()

    def dvalue(core):
        for i in range(2):
            head = 2 * core + i
            for g in range(GROUP):
                columns = pl.ds(pl.multiple_of((head * GROUP + g) * HEAD, HEAD), HEAD)
                douts[g * LEN:(g + 1) * LEN, :] = (coefv[...] * ogv[:, columns].astype(F32)).astype(BF16)
            piece = _nn(pt[head], douts[...]).astype(BF16)
            dvs[core, :, i * HEAD:(i + 1) * HEAD] = piece
            dvf[:, pl.ds(pl.multiple_of(head * HEAD, HEAD), HEAD)] = piece

    dv_copies = []

    def dvalue_other():
        dvalue(1 - c)
        dv_copies.append(send(dvs.at[1 - c], dvr, partner))

    def dvalue_own():
        dvalue(c)
        dvt[:, 0:LEN] = dvs[c].T

    def meet():
        dv_copies[0].wait_recv()
        dvt[:, LEN:2 * LEN] = dvr[...].T
        loads[2].wait()
        hidden_copy.wait_recv()

    def partial(yl, first, count):
        def one(i, carry):
            zz = zs(first + i)
            columns = pl.ds(pl.multiple_of((yl * 8 + zz) * 512, 512), 512)
            block = _nn(dvt[...], hv[:, columns]).astype(BF16)
            for i in range(N_X):
                b = block[:, i * 128:(i + 1) * 128]
                PA[yl, zz, i, 0] = b[0:32]
                PA[yl, zz, i, 1] = b[32:64]
                PB[yl, zz, i, 0] = b[64:96]
                PB[yl, zz, i, 1] = b[96:128]
                PC[yl, zz, i, 0] = b[128:192]
                PC[yl, zz, i, 1] = b[192:256]
            return carry

        lax.fori_loop(0, count, one, 0, unroll=True)

    def added(*terms):
        total = terms[0].astype(F32)
        for term in terms[1:]:
            total = total + term.astype(F32)
        return total

    def reduce_a(first, size):
        part = pl.ds(first, size)
        up = send(PA.at[:, :, xs(2), 0, part], rax.at[0, :, :, part], at_x(1))
        down = send(PA.at[:, :, xs(2), 1, part], rax.at[1, :, :, part], at_x(-1))
        up_b = send(PA.at[:, :, xs(1), 1, part], rax.at[2, :, :, part], at_x(1))
        down_b = send(PA.at[:, :, xs(-1), 0, part], rax.at[3, :, :, part], at_x(-1))
        yield
        up.wait_recv()
        PA[:, :, xs(1), 0, part] = added(PA[:, :, xs(1), 0, part], rax[0, :, :, part]).astype(BF16)
        up = send(PA.at[:, :, xs(1), 0, part], rax.at[4, :, :, part], at_x(1))
        down.wait_recv()
        PA[:, :, xs(-1), 1, part] = added(PA[:, :, xs(-1), 1, part], rax[1, :, :, part]).astype(BF16)
        down = send(PA.at[:, :, xs(-1), 1, part], rax.at[5, :, :, part], at_x(-1))
        yield
        up_b.wait_recv()
        down_b.wait_recv()
        up.wait_recv()
        down.wait_recv()
        PA[:, :, x, 0, part] = added(PA[:, :, x, 0, part], rax[3, :, :, part], rax[4, :, :, part]).astype(BF16)
        PA[:, :, x, 1, part] = added(PA[:, :, x, 1, part], rax[2, :, :, part], rax[5, :, :, part]).astype(BF16)
        copies = [send(PA.at[ys(d) % 2, :, x, ys(d) // 2, part], ray.at[d - 1, :, part], at_y(d)) for d in (2, 1, 3)]
        yield
        for copy in copies:
            copy.wait_recv()
        PA[y_lo, :, x, y_hi, part] = added(PA[y_lo, :, x, y_hi, part], ray[0, :, part], ray[1, :, part], ray[2, :, part]).astype(BF16)
        copies = [send(PA.at[y_lo, zs(d), x, y_hi, part], raz.at[d - 1, part], at_z(d)) for d in (4, 3, 5, 2, 6, 1, 7)]
        yield
        for copy in copies:
            copy.wait_recv()
        fin[y_hi, c, part] = added(PA[y_lo, z, x, y_hi, part], *[raz[i, part] for i in range(7)]).astype(BF16)

    def reduce_c(first, size):
        part = pl.ds(first, size)

        def view(d, h):
            return PC.at[ys(d) % 2, pl.ds(4 * h, 4), :, ys(d) // 2, part]

        def get(d, h):
            return PC[ys(d) % 2, pl.ds(4 * h, 4), :, ys(d) // 2, part]

        def put(d, h, value):
            PC[ys(d) % 2, pl.ds(4 * h, 4), :, ys(d) // 2, part] = value.astype(BF16)

        up = send(view(2, 0), rcy.at[0, :, :, part], at_y(1))
        down = send(view(2, 1), rcy.at[1, :, :, part], at_y(-1))
        yield
        up_b = send(view(1, 1), rcy.at[2, :, :, part], at_y(1))
        down_b = send(view(-1, 0), rcy.at[3, :, :, part], at_y(-1))
        yield
        up.wait_recv()
        put(1, 0, added(get(1, 0), rcy[0, :, :, part]))
        up = send(view(1, 0), rcy.at[4, :, :, part], at_y(1))
        down.wait_recv()
        put(-1, 1, added(get(-1, 1), rcy[1, :, :, part]))
        down = send(view(-1, 1), rcy.at[5, :, :, part], at_y(-1))
        yield
        up_b.wait_recv()
        down_b.wait_recv()
        up.wait_recv()
        down.wait_recv()
        put(0, 0, added(get(0, 0), rcy[3, :, :, part], rcy[4, :, :, part]))
        put(0, 1, added(get(0, 1), rcy[2, :, :, part], rcy[5, :, :, part]))
        copies = [send(PC.at[y_lo, :, xs(d), y_hi, part], rcx.at[d - 1, :, part], at_x(d)) for d in (2, 1, 3)]
        yield
        for copy in copies:
            copy.wait_recv()
        PC[y_lo, :, x, y_hi, part] = added(PC[y_lo, :, x, y_hi, part], rcx[0, :, part], rcx[1, :, part], rcx[2, :, part]).astype(BF16)
        copies = [send(PC.at[y_lo, zs(d), x, y_hi, part], rcz.at[d - 1, part], at_z(d)) for d in (4, 3, 5, 2, 6, 1, 7)]
        yield
        for copy in copies:
            copy.wait_recv()
        fin[y_hi, c, pl.ds(RA + RB + first, size)] = added(
            PC[y_lo, z, x, y_hi, part], *[rcz[i, part] for i in range(7)]
        ).astype(BF16)

    def reduce_b(first, size):
        part = pl.ds(first, size)
        up = send(PB.at[:, zs(4), :, 0, part], rbz.at[0, :, :, 0, part], at_z(1))
        down = send(PB.at[:, zs(4), :, 1, part], rbz.at[0, :, :, 1, part], at_z(-1))
        yield
        up.wait_recv()
        PB[:, zs(3), :, 0, part] = added(PB[:, zs(3), :, 0, part], rbz[0, :, :, 0, part]).astype(BF16)
        up = send(PB.at[:, zs(3), :, :, part], rbz.at[1, :, :, :, part], at_z(1))
        down.wait_recv()
        PB[:, zs(-3), :, 1, part] = added(PB[:, zs(-3), :, 1, part], rbz[0, :, :, 1, part]).astype(BF16)
        down = send(PB.at[:, zs(-3), :, :, part], rbz.at[2, :, :, :, part], at_z(-1))
        yield
        for d in (2, 1):
            up.wait_recv()
            PB[:, zs(d), :, :, part] = added(PB[:, zs(d), :, :, part], rbz[5 - 2 * d, :, :, :, part]).astype(BF16)
            up = send(PB.at[:, zs(d), :, :, part], rbz.at[7 - 2 * d, :, :, :, part], at_z(1))
            down.wait_recv()
            PB[:, zs(-d), :, :, part] = added(PB[:, zs(-d), :, :, part], rbz[6 - 2 * d, :, :, :, part]).astype(BF16)
            down = send(PB.at[:, zs(-d), :, :, part], rbz.at[8 - 2 * d, :, :, :, part], at_z(-1))
            yield
        up.wait_recv()
        down.wait_recv()
        PB[:, z, :, :, part] = added(PB[:, z, :, :, part], rbz[5, :, :, :, part], rbz[6, :, :, :, part]).astype(BF16)
        copies = [send(PB.at[:, z, xs(d), :, part], rbx.at[d - 1, :, :, part], at_x(d)) for d in (2, 1, 3)]
        yield
        for copy in copies:
            copy.wait_recv()
        PB[:, z, x, :, part] = added(PB[:, z, x, :, part], rbx[0, :, :, part], rbx[1, :, :, part], rbx[2, :, :, part]).astype(BF16)
        copies = [send(PB.at[ys(d) % 2, z, x, ys(d) // 2, part], rby.at[d - 1, part], at_y(d)) for d in (2, 1, 3)]
        yield
        for copy in copies:
            copy.wait_recv()
        fin[y_hi, c, pl.ds(RA + first, size)] = added(PB[y_lo, z, x, y_hi, part], rby[0, part], rby[1, part], rby[2, part]).astype(BF16)

    def product(yl, i):
        def one(t, carry):
            first = 4 * t
            rows = [W[h, yl, first + j, i] for j in range(4) for h in range(2)]
            block = _nt(dvf[...], jnp.concatenate(rows, axis=0)).astype(BF16)
            for j in range(4):
                at = ((yl * 8 + first + j) * 4 + i) * 128
                ig[:, pl.ds(pl.multiple_of(at, 128), 128)] = block[:, j * 128:(j + 1) * 128]
            return carry

        lax.fori_loop(0, 2, one, 0, unroll=True)

    products = []

    def product_next():
        n = len(products)
        place = n // 2
        group = (0, 1, 1, 2)[place]
        if n in (0, 2, 6):
            for key in ("B", "M", "A0", "C0") if n == 0 else ("A%d" % group, "C%d" % group):
                for copy in forwards[key]:
                    copy.wait_recv()
        product(n % 2, (x, xs(-1), xs(1), xs(2))[place])
        products.append(0)

    steps = {
        "stat": stats_steps(),
        "ga": gather_a(),
        "gb": gather_b(),
        "gc": gather_c(),
        "ra": reduce_a(0, RA),
        "rb": reduce_b(0, RB),
        "rc": reduce_c(0, 32),
        "rd": reduce_c(32, 32),
    }

    def partial_first():
        meet()
        partial(y_lo, 4, 1)
        partial(1 - y_lo, 4, 1)

    def partial_third():
        partial(1 - y_lo, 3, 1)
        partial(1 - y_lo, 5, 1)

    work = {
        "att": attend_next,
        "coef": make_coef,
        "pass2a": dvalue_other,
        "pass2b": dvalue_own,
        "part0": partial_first,
        "part1": lambda: partial(y_lo, 5, 7),
        "part2": partial_third,
        "part3": lambda: partial(1 - y_lo, 6, 5),
        "prod": product_next,
    }
    hidden_copy = send(hid, hv.at[pl.ds(LEN, LEN)], partner)
    loads[4].wait()
    for name in ORDER:
        if name in work:
            work[name]()
        else:
            advance([steps[name]])
    advance(list(steps.values()))
    while left(steps.values()):
        advance(list(steps.values()))

    mine = fin.at[y_hi, c]
    copies = [
        send(mine, mine, at_y(2)),
        send(mine, mine, partner),
        send(mine, mine, _device(x, ys(2), z, 1 - c)),
    ]
    for copy in copies:
        copy.wait_recv()
    pieces = []
    for core in range(2):
        for first, size in ((0, RA), (RA, RB), (RA + RB, RC)):
            for half in range(2):
                pieces.append(fin[half, core, pl.ds(first, size)])
    wg[...] = jnp.concatenate(pieces, axis=0).astype(F32).T

    for copy in sent:
        copy.wait_send()


def write_out(ig, wg, cf, ig_out, wg_out, cf_out, sem):
    rows = LEN // 8
    copies = [pltpu.make_async_copy(wg, wg_out, sem.at[8]), pltpu.make_async_copy(cf, cf_out, sem.at[9])]
    for i in range(8):
        part = pl.ds(i * rows, rows)
        copies.append(pltpu.make_async_copy(ig.at[part], ig_out.at[part], sem.at[i]))
    for copy in copies:
        copy.start()
    for copy in copies:
        copy.wait()


def local(
    hidden_in, value_weight, queries, keys, out_grad, new_logp, old_logp, rewards, resp_len, group_id
):
    vmem = pl.BlockSpec(memory_space=pltpu.VMEM)
    hbm = pl.BlockSpec(memory_space=pltpu.HBM)
    bf = functools.partial(pltpu.VMEM, dtype=BF16)
    scratch = [
        bf((2 * LEN, D)),
        bf((LEN, 4096)),
        bf((LEN, 4096)),
        bf((LEN, 512)),
        bf((KV_HEADS, LEN, GROUP * LEN)),
        bf((GROUP * LEN, HEAD)),
        bf((2, LEN, 256)),
        bf((LEN, 512)),
        bf((LEN, 256)),
        bf((256, 2 * LEN)),
        bf((2, 2, 8, 4, 64, 512)),
        bf((2, 8, 4, 2, RA, 128)),
        bf((2, 8, 4, 2, RB, 128)),
        bf((2, 8, 4, 2, RC, 128)),
        bf((6, 2, 8, RA, 128)),
        bf((3, 8, RA, 128)),
        bf((7, RA, 128)),
        bf((6, 4, 4, RC, 128)),
        bf((3, 8, RC, 128)),
        bf((7, RC, 128)),
        bf((7, 2, 4, 2, RB, 128)),
        bf((3, 2, 2, RB, 128)),
        bf((3, RB, 128)),
        bf((2, 2, 128, 128)),
        pltpu.VMEM((4, 8, 128), F32),
        pltpu.VMEM((7, 8, 128), F32),
        pltpu.VMEM((7, 8, 128), F32),
        pltpu.VMEM((3, 8, 128), F32),
        pltpu.VMEM((LEN, HEAD), F32),
        pltpu.SemaphoreType.DMA((SLOTS,)),
        pltpu.SemaphoreType.DMA((SLOTS,)),
        pltpu.SemaphoreType.DMA((10,)),
        pltpu.VMEM((1, LEN), F32),
        pltpu.VMEM((1, LEN), F32),
        pltpu.VMEM((1, 1), F32),
        pltpu.VMEM((1, 1), jnp.int32),
        pltpu.VMEM((1, 1), jnp.int32),
    ]
    input_grad, weight_grad, clip_frac = pl.pallas_call(
        kernel,
        out_shape=(
            pltpu.VMEM((LEN, D), BF16),
            pltpu.VMEM((128, 512), F32),
            pltpu.VMEM((1, 128), F32),
        ),
        in_specs=[hbm] * 10,
        out_specs=(vmem, vmem, vmem),
        scratch_shapes=scratch,
        compiler_params=pltpu.CompilerParams(
            collective_id=0, has_side_effects=True, vmem_limit_bytes=56 << 20
        ),
        name="value_backward",
    )(
        hidden_in, value_weight, queries, keys, out_grad,
        new_logp.reshape(1, LEN), old_logp.reshape(1, LEN), rewards.reshape(1, 1), resp_len, group_id,
    )
    input_grad, weight_grad, clip_frac = pl.pallas_call(
        write_out,
        out_shape=(
            jax.ShapeDtypeStruct((LEN, D), BF16),
            jax.ShapeDtypeStruct((128, 512), F32),
            jax.ShapeDtypeStruct((1, 128), F32),
        ),
        in_specs=[vmem, vmem, vmem],
        out_specs=(hbm, hbm, hbm),
        scratch_shapes=[pltpu.SemaphoreType.DMA((10,))],
        compiler_params=pltpu.CompilerParams(vmem_limit_bytes=4 << 20),
        name="write_out",
    )(input_grad, weight_grad, clip_frac)
    return input_grad, weight_grad, clip_frac[0, 0]


def solution(mesh):
    rows = P(("cuts", "fsdp"), None)
    flat = P(("cuts", "fsdp"))
    return jax.shard_map(
        local,
        mesh=mesh,
        in_specs=(
            rows, P("fsdp", None), rows, rows, rows, flat, flat, flat, P("cuts", "fsdp"), P("cuts", "fsdp"),
        ),
        out_specs=(rows, P("fsdp", None), P()),
        check_vma=False,
    )
```

```python
import functools

import jax
import jax.numpy as jnp
from jax import lax
from jax.experimental import pallas as pl
from jax.experimental.pallas import tpu as pltpu
from jax.sharding import PartitionSpec as P

HEAD = 128
KV_HEADS = 4
GROUP = 8
LEN = 256
D = 8192
F32 = jnp.float32
BF16 = jnp.bfloat16
MESH = pl.DeviceIdType.MESH
N_X, N_Y, N_Z = 4, 4, 8
RA, RB, RC = 32, 32, 64
SLOTS = 192
ORDER = (
    "stat", "ga", "gb", "gc", "att", "att", "att", "att", "ga", "att",
    "att", "gb", "att", "stat", "gc", "att", "gb", "ga", "gc", "stat",
    "coef", "pass2a", "pass2b", "part0", "rb", "gb", "part1", "rc", "ga", "part2",
    "part3", "ra", "gc", "rc", "rb", "rd", "rd", "gb", "rc", "rb",
    "ga", "gb", "ra", "rb", "gb", "rd", "gc", "gc", "gc", "rb",
    "ga", "ra", "prod", "rc", "prod", "prod", "rb", "prod", "prod", "rd",
    "prod", "prod", "gc", "rc", "prod", "prod", "ra", "prod", "prod", "rd",
    "prod", "prod", "rb", "prod", "prod", "rc", "ra", "prod", "rd",
)


def _coords():
    cuts = lax.axis_index("cuts")
    fsdp = lax.axis_index("fsdp")
    core = cuts % 2
    y_hi = cuts // 2
    y_lo = fsdp // 32
    z = (fsdp // 4) % 8
    x = fsdp % 4
    return x, y_hi * 2 + y_lo, z, core


def _device(x, y, z, core):
    return ((y // 2) * 2 + core, (y % 2) * 32 + z * 4 + x)


def _nt(a, b):
    return lax.dot_general(a, b, (((1,), (1,)), ((), ())), preferred_element_type=F32)


def _nn(a, b):
    return lax.dot_general(a, b, (((1,), (0,)), ((), ())), preferred_element_type=F32)


def kernel(
    hid, w, q, k, og, nlp, olp, rew, rlen, gid,
    ig, wg, cf,
    hv, qv, ogv, kv, pt, douts, dvs, dvf, dvr, dvt, W,
    PA, PB, PC, rax, ray, raz, rcy, rcx, rcz, rbz, rbx, rby,
    fin, st, rsp, rsz, rsc, coefv,
    ssem, rsem, lsem, nlv, olv, rwv, rlv, giv,
):
    x, y, z, c = _coords()
    y_lo, y_hi = y % 2, y // 2

    def xs(d):
        return (x + d + N_X) % N_X

    def ys(d):
        return (y + d + N_Y) % N_Y

    def zs(d):
        return (z + d + N_Z) % N_Z

    def at_x(d):
        return _device(xs(d), y, z, c)

    def at_y(d):
        return _device(x, ys(d), z, c)

    def at_z(d):
        return _device(x, y, zs(d), c)

    partner = _device(x, y, z, 1 - c)
    sent = []

    def send(src, dst, device):
        i = len(sent)
        copy = pltpu.make_async_remote_copy(
            src_ref=src, dst_ref=dst, send_sem=ssem.at[i], recv_sem=rsem.at[i],
            device_id=device, device_id_type=MESH,
        )
        copy.start()
        sent.append(copy)
        return copy

    loads = [
        pltpu.make_async_copy(q, qv, lsem.at[0]),
        pltpu.make_async_copy(og, ogv, lsem.at[1]),
        pltpu.make_async_copy(hid, hv.at[pl.ds(0, LEN)], lsem.at[2]),
        pltpu.make_async_copy(k, kv, lsem.at[3]),
        pltpu.make_async_copy(
            w.at[pl.ds(pl.multiple_of(64 * c, 64), 64)], W.at[c, y_lo, z, x], lsem.at[4]
        ),
    ]
    for i, (src, dst) in enumerate(((nlp, nlv), (olp, olv), (rew, rwv), (rlen, rlv), (gid, giv))):
        loads.append(pltpu.make_async_copy(src, dst, lsem.at[5 + i]))
    for i in (5, 6, 7, 8, 9, 4, 3, 0, 1, 2):
        loads[i].start()

    barrier = pltpu.get_barrier_semaphore()
    around = [at_x(1), at_x(-1), at_x(2), at_y(1), at_y(-1), at_y(2), partner]
    around += [at_z(d) for d in range(1, 8)]
    around += [_device(x, ys(2), z, 1 - c)]
    flip = y_hi * 2 + (1 - y_lo)
    around += [_device(xs(d), flip, z, c) for d in range(1, 4)]
    for device in around:
        pl.semaphore_signal(barrier, inc=1, device_id=device, device_id_type=MESH)

    for load in loads[5:]:
        load.wait()
    lane = lax.broadcasted_iota(jnp.int32, (8, 128), 1)
    group = giv[...]
    reward = rwv[...]
    length = rlv[...].astype(F32)
    position = lax.broadcasted_iota(jnp.int32, (1, LEN), 1)
    live = (position < rlv[...]).astype(F32)
    ratio = jnp.exp(nlv[...] - olv[...])
    outside = jnp.logical_or(ratio > 1.28, ratio < 0.8).astype(F32)
    clipped = jnp.sum(live * outside, axis=1, keepdims=True)
    member = (lane % 8 == group).astype(F32)
    stats = jnp.where(
        lane < 8, member,
        jnp.where(
            lane < 16, member * reward,
            jnp.where(
                lane < 24, member * (reward * reward),
                jnp.where(lane == 24, length, jnp.where(lane == 25, clipped, 0.0)),
            ),
        ),
    )
    st[0] = stats
    pl.semaphore_wait(barrier, len(around))

    def stats_steps():
        copies = [send(st.at[0], rsz.at[d - 1], at_z(d)) for d in (4, 3, 5, 2, 6, 1, 7)]
        yield
        for copy in copies:
            copy.wait_recv()
        total = st[0]
        for i in range(7):
            total = total + rsz[i]
        st[1] = total
        plane = [(d, to) for d in (2, 1, 3) for to in (flip, y)] + [(0, flip)]
        copies = [send(st.at[1], rsp.at[i], _device(xs(d), to, z, c)) for i, (d, to) in enumerate(plane)]
        yield
        for copy in copies:
            copy.wait_recv()
        total = st[1]
        for i in range(7):
            total = total + rsp[i]
        st[3] = total
        copies = [
            send(st.at[3], rsc.at[0], at_y(2)),
            send(st.at[3], rsc.at[1], partner),
            send(st.at[3], rsc.at[2], _device(x, ys(2), z, 1 - c)),
        ]
        yield
        for copy in copies:
            copy.wait_recv()
        every = ((st[3] + rsc[0]) + (rsc[1] + rsc[2]))[0:1]
        top = lane[0:1]
        all_live = jnp.sum(jnp.where(top == 24, every, 0.0), axis=1, keepdims=True)
        all_out = jnp.sum(jnp.where(top == 25, every, 0.0), axis=1, keepdims=True)
        cf[...] = jnp.broadcast_to(all_out / all_live, (1, 128))

    def ring_z(view, half):
        up = send(view(z), view(z), at_z(1))
        down = send(view(z), view(z), at_z(-1))
        yield
        for d in (1, 2, 3):
            up.wait_recv()
            down.wait_recv()
            if d < 3:
                up = send(view(zs(-d)), view(zs(-d)), at_z(1))
                down = send(view(zs(d)), view(zs(d)), at_z(-1))
            else:
                up = send(half(zs(-3), 0), half(zs(-3), 0), at_z(1))
                down = send(half(zs(3), 1), half(zs(3), 1), at_z(-1))
            yield
        up.wait_recv()
        down.wait_recv()

    def near_z(view, half):
        copies = [send(view(z), view(z), at_z(d)) for d in (2, -2, 1, -1)]
        yield
        for copy in copies:
            copy.wait_recv()
        below, above = zs(-2), zs(2)
        copies = [
            send(half(below, 0), half(below, 0), at_z(2)),
            send(half(above, 1), half(above, 1), at_z(-2)),
            send(view(below), view(below), at_z(1)),
            send(view(above), view(above), at_z(-1)),
        ]
        yield
        for copy in copies:
            copy.wait_recv()

    forwards = {}

    def forward(key, ref):
        forwards.setdefault(key, []).append(send(ref, ref, partner))

    def gather_a():
        own = W.at[c, y_lo, z, x, pl.ds(0, 16)]
        copy = send(own, own, at_y(1))
        yield
        copy.wait_recv()
        yield from near_z(
            lambda i: W.at[c, :, i, x, pl.ds(0, 16)],
            lambda i, h: W.at[c, h, i, x, pl.ds(0, 16)],
        )

        def view(i):
            return W.at[c, :, :, i, pl.ds(0, 16)]

        def half(i, h):
            return W.at[c, h, :, i, pl.ds(0, 16)]

        up = send(view(x), view(x), at_x(1))
        down = send(view(x), view(x), at_x(-1))
        forward("A0", view(x))
        yield
        up.wait_recv()
        down.wait_recv()
        up = send(half(xs(-1), 0), half(xs(-1), 0), at_x(1))
        down = send(half(xs(1), 1), half(xs(1), 1), at_x(-1))
        forward("A1", view(xs(-1)))
        forward("A1", view(xs(1)))
        yield
        up.wait_recv()
        down.wait_recv()
        forward("A2", view(xs(2)))

    def gather_b():
        own = W.at[c, y_lo, z, x, pl.ds(16, 16)]
        copies = [send(own, own, at_x(d)) for d in (1, 2, 3)]
        yield
        for copy in copies:
            copy.wait_recv()
        left = W.at[c, y_lo, z, pl.ds(0, 2), pl.ds(16, 16)]
        right = W.at[c, y_lo, z, pl.ds(2, 2), pl.ds(16, 16)]
        copies = [send(left, left, at_y(1)), send(right, right, at_y(-1))]
        yield
        for copy in copies:
            copy.wait_recv()
        def view(i):
            return W.at[c, :, i, :, pl.ds(16, 16)]

        yield from ring_z(view, lambda i, h: W.at[c, h, i, :, pl.ds(16, 16)])
        whole = W.at[c, :, :, :, pl.ds(16, 16)]
        forward("B", whole)

    def gather_c():
        yield from near_z(
            lambda i: W.at[c, y_lo, i, x, pl.ds(32, 32)],
            lambda i, h: W.at[c, y_lo, i, x, pl.ds(32 + 16 * h, 16)],
        )
        final = []

        def view(i):
            return W.at[c, y_lo, :, i, pl.ds(32, 32)]

        def half(i, h):
            return W.at[c, y_lo, pl.ds(4 * h, 4), i, pl.ds(32, 32)]

        def across(i):
            final.append(send(half(i, 0), half(i, 0), at_y(1)))
            final.append(send(half(i, 1), half(i, 1), at_y(-1)))

        up = send(view(x), view(x), at_x(1))
        down = send(view(x), view(x), at_x(-1))
        across(x)
        yield
        up.wait_recv()
        down.wait_recv()
        up = send(half(xs(-1), 0), half(xs(-1), 0), at_x(1))
        down = send(half(xs(1), 1), half(xs(1), 1), at_x(-1))
        across(xs(-1))
        across(xs(1))
        yield
        up.wait_recv()
        down.wait_recv()
        across(xs(2))
        forward("M", W.at[c, y_lo, :, :, pl.ds(32, 32)])
        yield
        for key, copies, places in (
            ("C0", final[0:2], (x,)),
            ("C1", final[2:6], (xs(-1), xs(1))),
            ("C2", final[6:8], (xs(2),)),
        ):
            for copy in copies:
                copy.wait_recv()
            for i in places:
                forward(key, W.at[c, 1 - y_lo, :, i, pl.ds(32, 32)])
            yield

    done = []

    def advance(steps):
        for step in steps:
            if step not in done and next(step, "end") == "end":
                done.append(step)

    def left(*lists):
        return any(step not in done for steps in lists for step in steps)

    factor = (1.0 / HEAD**0.5) * 1.4426950408889634
    row = lax.broadcasted_iota(jnp.int32, (HEAD, HEAD), 0)
    col = lax.broadcasted_iota(jnp.int32, (HEAD, HEAD), 1)
    causal = row <= col

    def soft(scores):
        top = jnp.max(scores, axis=0, keepdims=True)
        expo = jnp.exp2((scores - top) * factor)
        return (expo * (1.0 / jnp.sum(expo, axis=0, keepdims=True))).astype(BF16)

    def attend(head, first):
        keys = kv[:, head * HEAD:(head + 1) * HEAD]

        def one(i, carry):
            g = first + i
            n = head * GROUP + g
            query = qv[:, pl.ds(pl.multiple_of(n * HEAD, HEAD), HEAD)]
            early = jnp.where(causal, _nt(keys[:128], query[:128]), -1e30)
            late = _nt(keys, query[128:])
            late = jnp.concatenate([late[:128], jnp.where(causal, late[128:], -1e30)], axis=0)
            at = pl.multiple_of(g * LEN, LEN)
            pt[head, pl.ds(0, 128), pl.ds(at, 128)] = soft(early)
            pt[head, pl.ds(128, 128), pl.ds(at, 128)] = jnp.zeros((128, 128), BF16)
            pt[head, :, pl.ds(at + 128, 128)] = soft(late)
            return carry

        lax.fori_loop(0, 4, one, 0, unroll=2)

    attended = []

    def attend_next():
        if not attended:
            loads[3].wait()
            loads[0].wait()
        attend(len(attended) // 2, 4 * (len(attended) % 2))
        attended.append(0)

    def make_coef():
        slice_total = st[3][0:1]
        top = lane[0:1]

        def pick(at):
            return jnp.sum(jnp.where(top == at, slice_total, 0.0), axis=1, keepdims=True)

        own_cnt, own_one, own_two = pick(group), pick(8 + group), pick(16 + group)
        mean = own_one / own_cnt
        var = own_two / own_cnt - mean * mean
        adv = (reward - mean) / jnp.sqrt(var + 0.25)
        total = pick(24) * 4.0
        active = jnp.where(adv > 0, (ratio < 1.28).astype(F32), (ratio > 0.8).astype(F32))
        coef = -live * adv * ratio * active * (65536.0 / total)
        square = (LEN, LEN)
        diagonal = lax.broadcasted_iota(jnp.int32, square, 0) == lax.broadcasted_iota(jnp.int32, square, 1)
        coefv[...] = jnp.broadcast_to(
            jnp.sum(jnp.where(diagonal, coef, 0.0), axis=1, keepdims=True), (LEN, HEAD)
        )
        loads[1].wait()

    def dvalue(core):
        for i in range(2):
            head = 2 * core + i
            for g in range(GROUP):
                columns = pl.ds(pl.multiple_of((head * GROUP + g) * HEAD, HEAD), HEAD)
                douts[g * LEN:(g + 1) * LEN, :] = (coefv[...] * ogv[:, columns].astype(F32)).astype(BF16)
            piece = _nn(pt[head], douts[...]).astype(BF16)
            dvs[core, :, i * HEAD:(i + 1) * HEAD] = piece
            dvf[:, pl.ds(pl.multiple_of(head * HEAD, HEAD), HEAD)] = piece

    dv_copies = []

    def dvalue_other():
        dvalue(1 - c)
        dv_copies.append(send(dvs.at[1 - c], dvr, partner))

    def dvalue_own():
        dvalue(c)
        dvt[:, 0:LEN] = dvs[c].T

    def meet():
        dv_copies[0].wait_recv()
        dvt[:, LEN:2 * LEN] = dvr[...].T
        loads[2].wait()
        hidden_copy.wait_recv()

    def partial(yl, first, count):
        def one(i, carry):
            zz = zs(first + i)
            columns = pl.ds(pl.multiple_of((yl * 8 + zz) * 512, 512), 512)
            block = _nn(dvt[...], hv[:, columns]).astype(BF16)
            for i in range(N_X):
                b = block[:, i * 128:(i + 1) * 128]
                PA[yl, zz, i, 0] = b[0:32]
                PA[yl, zz, i, 1] = b[32:64]
                PB[yl, zz, i, 0] = b[64:96]
                PB[yl, zz, i, 1] = b[96:128]
                PC[yl, zz, i, 0] = b[128:192]
                PC[yl, zz, i, 1] = b[192:256]
            return carry

        lax.fori_loop(0, count, one, 0, unroll=True)

    def added(*terms):
        total = terms[0].astype(F32)
        for term in terms[1:]:
            total = total + term.astype(F32)
        return total

    def reduce_a(first, size):
        part = pl.ds(first, size)
        up = send(PA.at[:, :, xs(2), 0, part], rax.at[0, :, :, part], at_x(1))
        down = send(PA.at[:, :, xs(2), 1, part], rax.at[1, :, :, part], at_x(-1))
        up_b = send(PA.at[:, :, xs(1), 1, part], rax.at[2, :, :, part], at_x(1))
        down_b = send(PA.at[:, :, xs(-1), 0, part], rax.at[3, :, :, part], at_x(-1))
        yield
        up.wait_recv()
        PA[:, :, xs(1), 0, part] = added(PA[:, :, xs(1), 0, part], rax[0, :, :, part]).astype(BF16)
        up = send(PA.at[:, :, xs(1), 0, part], rax.at[4, :, :, part], at_x(1))
        down.wait_recv()
        PA[:, :, xs(-1), 1, part] = added(PA[:, :, xs(-1), 1, part], rax[1, :, :, part]).astype(BF16)
        down = send(PA.at[:, :, xs(-1), 1, part], rax.at[5, :, :, part], at_x(-1))
        yield
        up_b.wait_recv()
        down_b.wait_recv()
        up.wait_recv()
        down.wait_recv()
        PA[:, :, x, 0, part] = added(PA[:, :, x, 0, part], rax[3, :, :, part], rax[4, :, :, part]).astype(BF16)
        PA[:, :, x, 1, part] = added(PA[:, :, x, 1, part], rax[2, :, :, part], rax[5, :, :, part]).astype(BF16)
        copies = [send(PA.at[ys(d) % 2, :, x, ys(d) // 2, part], ray.at[d - 1, :, part], at_y(d)) for d in (2, 1, 3)]
        yield
        for copy in copies:
            copy.wait_recv()
        PA[y_lo, :, x, y_hi, part] = added(PA[y_lo, :, x, y_hi, part], ray[0, :, part], ray[1, :, part], ray[2, :, part]).astype(BF16)
        copies = [send(PA.at[y_lo, zs(d), x, y_hi, part], raz.at[d - 1, part], at_z(d)) for d in (4, 3, 5, 2, 6, 1, 7)]
        yield
        for copy in copies:
            copy.wait_recv()
        fin[y_hi, c, part] = added(PA[y_lo, z, x, y_hi, part], *[raz[i, part] for i in range(7)]).astype(BF16)

    def reduce_c(first, size):
        part = pl.ds(first, size)

        def view(d, h):
            return PC.at[ys(d) % 2, pl.ds(4 * h, 4), :, ys(d) // 2, part]

        def get(d, h):
            return PC[ys(d) % 2, pl.ds(4 * h, 4), :, ys(d) // 2, part]

        def put(d, h, value):
            PC[ys(d) % 2, pl.ds(4 * h, 4), :, ys(d) // 2, part] = value.astype(BF16)

        up = send(view(2, 0), rcy.at[0, :, :, part], at_y(1))
        down = send(view(2, 1), rcy.at[1, :, :, part], at_y(-1))
        yield
        up_b = send(view(1, 1), rcy.at[2, :, :, part], at_y(1))
        down_b = send(view(-1, 0), rcy.at[3, :, :, part], at_y(-1))
        yield
        up.wait_recv()
        put(1, 0, added(get(1, 0), rcy[0, :, :, part]))
        up = send(view(1, 0), rcy.at[4, :, :, part], at_y(1))
        down.wait_recv()
        put(-1, 1, added(get(-1, 1), rcy[1, :, :, part]))
        down = send(view(-1, 1), rcy.at[5, :, :, part], at_y(-1))
        yield
        up_b.wait_recv()
        down_b.wait_recv()
        up.wait_recv()
        down.wait_recv()
        put(0, 0, added(get(0, 0), rcy[3, :, :, part], rcy[4, :, :, part]))
        put(0, 1, added(get(0, 1), rcy[2, :, :, part], rcy[5, :, :, part]))
        copies = [send(PC.at[y_lo, :, xs(d), y_hi, part], rcx.at[d - 1, :, part], at_x(d)) for d in (2, 1, 3)]
        yield
        for copy in copies:
            copy.wait_recv()
        PC[y_lo, :, x, y_hi, part] = added(PC[y_lo, :, x, y_hi, part], rcx[0, :, part], rcx[1, :, part], rcx[2, :, part]).astype(BF16)
        copies = [send(PC.at[y_lo, zs(d), x, y_hi, part], rcz.at[d - 1, part], at_z(d)) for d in (4, 3, 5, 2, 6, 1, 7)]
        yield
        for copy in copies:
            copy.wait_recv()
        fin[y_hi, c, pl.ds(RA + RB + first, size)] = added(
            PC[y_lo, z, x, y_hi, part], *[rcz[i, part] for i in range(7)]
        ).astype(BF16)

    def reduce_b(first, size):
        part = pl.ds(first, size)
        up = send(PB.at[:, zs(4), :, 0, part], rbz.at[0, :, :, 0, part], at_z(1))
        down = send(PB.at[:, zs(4), :, 1, part], rbz.at[0, :, :, 1, part], at_z(-1))
        yield
        up.wait_recv()
        PB[:, zs(3), :, 0, part] = added(PB[:, zs(3), :, 0, part], rbz[0, :, :, 0, part]).astype(BF16)
        up = send(PB.at[:, zs(3), :, :, part], rbz.at[1, :, :, :, part], at_z(1))
        down.wait_recv()
        PB[:, zs(-3), :, 1, part] = added(PB[:, zs(-3), :, 1, part], rbz[0, :, :, 1, part]).astype(BF16)
        down = send(PB.at[:, zs(-3), :, :, part], rbz.at[2, :, :, :, part], at_z(-1))
        yield
        for d in (2, 1):
            up.wait_recv()
            PB[:, zs(d), :, :, part] = added(PB[:, zs(d), :, :, part], rbz[5 - 2 * d, :, :, :, part]).astype(BF16)
            up = send(PB.at[:, zs(d), :, :, part], rbz.at[7 - 2 * d, :, :, :, part], at_z(1))
            down.wait_recv()
            PB[:, zs(-d), :, :, part] = added(PB[:, zs(-d), :, :, part], rbz[6 - 2 * d, :, :, :, part]).astype(BF16)
            down = send(PB.at[:, zs(-d), :, :, part], rbz.at[8 - 2 * d, :, :, :, part], at_z(-1))
            yield
        up.wait_recv()
        down.wait_recv()
        PB[:, z, :, :, part] = added(PB[:, z, :, :, part], rbz[5, :, :, :, part], rbz[6, :, :, :, part]).astype(BF16)
        copies = [send(PB.at[:, z, xs(d), :, part], rbx.at[d - 1, :, :, part], at_x(d)) for d in (2, 1, 3)]
        yield
        for copy in copies:
            copy.wait_recv()
        PB[:, z, x, :, part] = added(PB[:, z, x, :, part], rbx[0, :, :, part], rbx[1, :, :, part], rbx[2, :, :, part]).astype(BF16)
        copies = [send(PB.at[ys(d) % 2, z, x, ys(d) // 2, part], rby.at[d - 1, part], at_y(d)) for d in (2, 1, 3)]
        yield
        for copy in copies:
            copy.wait_recv()
        fin[y_hi, c, pl.ds(RA + first, size)] = added(PB[y_lo, z, x, y_hi, part], rby[0, part], rby[1, part], rby[2, part]).astype(BF16)

    def product(yl, first, i):
        rows = [W[h, yl, first + j, i] for j in range(4) for h in range(2)]
        block = _nt(dvf[...], jnp.concatenate(rows, axis=0)).astype(BF16)
        for j in range(4):
            at = ((yl * 8 + first + j) * 4 + i) * 128
            ig[:, pl.ds(pl.multiple_of(at, 128), 128)] = block[:, j * 128:(j + 1) * 128]

    products = []

    def product_next():
        n = len(products)
        place = n // 4
        group = (0, 1, 1, 2)[place]
        if n in (0, 4, 12):
            for key in ("B", "M", "A0", "C0") if n == 0 else ("A%d" % group, "C%d" % group):
                for copy in forwards[key]:
                    copy.wait_recv()
        product(n // 2 % 2, 4 * (n % 2), (x, xs(-1), xs(1), xs(2))[place])
        products.append(0)

    steps = {
        "stat": stats_steps(),
        "ga": gather_a(),
        "gb": gather_b(),
        "gc": gather_c(),
        "ra": reduce_a(0, RA),
        "rb": reduce_b(0, RB),
        "rc": reduce_c(0, 32),
        "rd": reduce_c(32, 32),
    }

    def partial_first():
        meet()
        partial(y_lo, 4, 1)
        partial(1 - y_lo, 4, 1)

    def partial_third():
        partial(1 - y_lo, 3, 1)
        partial(1 - y_lo, 5, 1)

    work = {
        "att": attend_next,
        "coef": make_coef,
        "pass2a": dvalue_other,
        "pass2b": dvalue_own,
        "part0": partial_first,
        "part1": lambda: partial(y_lo, 5, 7),
        "part2": partial_third,
        "part3": lambda: partial(1 - y_lo, 6, 5),
        "prod": product_next,
    }
    hidden_copy = send(hid, hv.at[pl.ds(LEN, LEN)], partner)
    loads[4].wait()
    for name in ORDER:
        if name in work:
            work[name]()
        else:
            advance([steps[name]])
    advance(list(steps.values()))
    while left(steps.values()):
        advance(list(steps.values()))

    mine = fin.at[y_hi, c]
    copies = [
        send(mine, mine, at_y(2)),
        send(mine, mine, partner),
        send(mine, mine, _device(x, ys(2), z, 1 - c)),
    ]
    for copy in copies:
        copy.wait_recv()
    pieces = []
    for core in range(2):
        for first, size in ((0, RA), (RA, RB), (RA + RB, RC)):
            for half in range(2):
                pieces.append(fin[half, core, pl.ds(first, size)])
    wg[...] = jnp.concatenate(pieces, axis=0).astype(F32).T

    for copy in sent:
        copy.wait_send()


def write_out(ig, wg, cf, ig_out, wg_out, cf_out, sem):
    rows = LEN // 8
    copies = [pltpu.make_async_copy(wg, wg_out, sem.at[8]), pltpu.make_async_copy(cf, cf_out, sem.at[9])]
    for i in range(8):
        part = pl.ds(i * rows, rows)
        copies.append(pltpu.make_async_copy(ig.at[part], ig_out.at[part], sem.at[i]))
    for copy in copies:
        copy.start()
    for copy in copies:
        copy.wait()


def local(
    hidden_in, value_weight, queries, keys, out_grad, new_logp, old_logp, rewards, resp_len, group_id
):
    vmem = pl.BlockSpec(memory_space=pltpu.VMEM)
    hbm = pl.BlockSpec(memory_space=pltpu.HBM)
    bf = functools.partial(pltpu.VMEM, dtype=BF16)
    scratch = [
        bf((2 * LEN, D)),
        bf((LEN, 4096)),
        bf((LEN, 4096)),
        bf((LEN, 512)),
        bf((KV_HEADS, LEN, GROUP * LEN)),
        bf((GROUP * LEN, HEAD)),
        bf((2, LEN, 256)),
        bf((LEN, 512)),
        bf((LEN, 256)),
        bf((256, 2 * LEN)),
        bf((2, 2, 8, 4, 64, 512)),
        bf((2, 8, 4, 2, RA, 128)),
        bf((2, 8, 4, 2, RB, 128)),
        bf((2, 8, 4, 2, RC, 128)),
        bf((6, 2, 8, RA, 128)),
        bf((3, 8, RA, 128)),
        bf((7, RA, 128)),
        bf((6, 4, 4, RC, 128)),
        bf((3, 8, RC, 128)),
        bf((7, RC, 128)),
        bf((7, 2, 4, 2, RB, 128)),
        bf((3, 2, 2, RB, 128)),
        bf((3, RB, 128)),
        bf((2, 2, 128, 128)),
        pltpu.VMEM((4, 8, 128), F32),
        pltpu.VMEM((7, 8, 128), F32),
        pltpu.VMEM((7, 8, 128), F32),
        pltpu.VMEM((3, 8, 128), F32),
        pltpu.VMEM((LEN, HEAD), F32),
        pltpu.SemaphoreType.DMA((SLOTS,)),
        pltpu.SemaphoreType.DMA((SLOTS,)),
        pltpu.SemaphoreType.DMA((10,)),
        pltpu.VMEM((1, LEN), F32),
        pltpu.VMEM((1, LEN), F32),
        pltpu.VMEM((1, 1), F32),
        pltpu.VMEM((1, 1), jnp.int32),
        pltpu.VMEM((1, 1), jnp.int32),
    ]
    input_grad, weight_grad, clip_frac = pl.pallas_call(
        kernel,
        out_shape=(
            pltpu.VMEM((LEN, D), BF16),
            pltpu.VMEM((128, 512), F32),
            pltpu.VMEM((1, 128), F32),
        ),
        in_specs=[hbm] * 10,
        out_specs=(vmem, vmem, vmem),
        scratch_shapes=scratch,
        compiler_params=pltpu.CompilerParams(
            collective_id=0, has_side_effects=True, vmem_limit_bytes=56 << 20
        ),
        name="value_backward",
    )(
        hidden_in, value_weight, queries, keys, out_grad,
        new_logp.reshape(1, LEN), old_logp.reshape(1, LEN), rewards.reshape(1, 1), resp_len, group_id,
    )
    input_grad, weight_grad, clip_frac = pl.pallas_call(
        write_out,
        out_shape=(
            jax.ShapeDtypeStruct((LEN, D), BF16),
            jax.ShapeDtypeStruct((128, 512), F32),
            jax.ShapeDtypeStruct((1, 128), F32),
        ),
        in_specs=[vmem, vmem, vmem],
        out_specs=(hbm, hbm, hbm),
        scratch_shapes=[pltpu.SemaphoreType.DMA((10,))],
        compiler_params=pltpu.CompilerParams(vmem_limit_bytes=4 << 20),
        name="write_out",
    )(input_grad, weight_grad, clip_frac)
    return input_grad, weight_grad, clip_frac[0, 0]


def solution(mesh):
    rows = P(("cuts", "fsdp"), None)
    flat = P(("cuts", "fsdp"))
    return jax.shard_map(
        local,
        mesh=mesh,
        in_specs=(
            rows, P("fsdp", None), rows, rows, rows, flat, flat, flat, P("cuts", "fsdp"), P("cuts", "fsdp"),
        ),
        out_specs=(rows, P("fsdp", None), P()),
        check_vma=False,
    )
```
